256 devices in a mesh: lon: 64 (over z, y, x_hi), spc: 4 (over x_lo, core).
Axes of the slice: x: 4 (x_hi: 2, x_lo: 2; x = x_hi * 2 + x_lo), y: 4, z: 8, core: 2. Of those that a mesh axis runs over, the one named last changes fastest.
Arguments:
- compound_group_loads: float32 [40, 9, 4, 1024, 128], P('spc', None, None, 'lon'), may hold values from 0.01 to 1
- leftover_stepfrac: float32 [4, 1024, 128], P('spc', 'lon'), may hold values from 0 to 1
- thermal_kelvins: float32 [4, 1024, 128], P('spc', 'lon'), may hold values from 250 to 310
- diffusive_numbers: float32 [3, 1024, 128], P(None, 'lon'), may hold values from 0.1 to 10
- whole_shifts: int32 [128], replicated, may hold values from 0 to 31, as said below
Outputs:
- particle: float32 [40, 9, 4, 1024, 128], P('spc', None, None, 'lon')
- zonal_flux: float32 [40, 4, 1024, 128], P('spc', None, 'lon')
The draws below stay inside these ranges and needn't reach their ends.
Inputs may be any that keep to these rules, and one draw needn't show every extreme that they name: `whole_shifts`: rows 32 and beyond have offsets of at most 15. Row 0 takes 31 and row 32 takes 16 - 1.
All inputs are finite; a program needn't handle non-finite values.
Results may differ from the reference program's by a relative error of at most 0.0001.
Values sent between devices are 32-bit elements; how exact they have to be, the bound alone decides.
No kernel may reach another device: no remote copies, remote signals or barrier semaphores. Data moves between devices by JAX's collectives and lax.ppermute only.
A program may use at most 64 MiB of HBM per device.

```python
import math
import jax
import jax.numpy as jnp
from jax import lax

SPECIES = 40
BINS = 9
STACK_HEIGHT = 4
MERIDIAN_LINES = 128
POLAR = 32
PITERS = 2
LON_DEV = 16
GIRDLE_BOXES = 1024
KMAX = 31


def draw_whole_shifts(key, part):
    row_index = jnp.arange(MERIDIAN_LINES, dtype=jnp.int32)
    ceiling = jnp.where(row_index < POLAR, KMAX, LON_DEV - 1).astype(jnp.int32)
    raw_bits = jax.random.randint(key, (MERIDIAN_LINES,), 0, 1 << 20, dtype=jnp.int32)
    drawn = raw_bits % (ceiling + 1)
    drawn = jnp.where(row_index == 0, KMAX, drawn)
    drawn = jnp.where(row_index == POLAR, LON_DEV - 1, drawn)
    return drawn.astype(jnp.int32)


def level_of(stream_key, shape, split, low, top_value):
    loudness = 1.0
    for axis_at, parts in split:
        draws = jax.random.uniform(jax.random.fold_in(jax.random.fold_in(stream_key, 6), axis_at), (parts,), jnp.float32, low / len(split), top_value / len(split))
        loudness = loudness * jnp.repeat(jnp.exp(draws), shape[axis_at] // parts).reshape((-1,) + (1,) * (len(shape) - 1 - axis_at))
    return loudness


def setup_inputs(seed: int = 0) -> dict:
    splits = jax.random.split(jax.random.key(seed), 6)
    return {
        "compound_group_loads": jnp.clip(jnp.exp(math.log(1.0) - 4.6051702 * jax.random.uniform(splits[0], (SPECIES, BINS, STACK_HEIGHT, GIRDLE_BOXES, MERIDIAN_LINES), jnp.float32) ** level_of(splits[0], (SPECIES, BINS, STACK_HEIGHT, GIRDLE_BOXES, MERIDIAN_LINES), ((0, 4), (3, 64)), -0.2, 0.2)), 0.01, 1.0),
        "leftover_stepfrac": jnp.clip(1.0 * jax.random.uniform(splits[1], (STACK_HEIGHT, GIRDLE_BOXES, MERIDIAN_LINES), jnp.float32) ** level_of(splits[1], (STACK_HEIGHT, GIRDLE_BOXES, MERIDIAN_LINES), ((0, 4), (1, 64)), -0.2, 0.2), 0.0, 1.0),
        "thermal_kelvins": jnp.clip(250.0 + 60.0 * jax.random.uniform(splits[2], (STACK_HEIGHT, GIRDLE_BOXES, MERIDIAN_LINES), jnp.float32) ** level_of(splits[2], (STACK_HEIGHT, GIRDLE_BOXES, MERIDIAN_LINES), ((0, 4), (1, 64)), -0.2, 0.2), 250.0, 310.0),
        "diffusive_numbers": jnp.clip(jnp.exp(math.log(10.0) - 4.6051702 * jax.random.uniform(splits[3], (STACK_HEIGHT - 1, GIRDLE_BOXES, MERIDIAN_LINES), jnp.float32) ** level_of(splits[3], (STACK_HEIGHT - 1, GIRDLE_BOXES, MERIDIAN_LINES), ((1, 64),), -0.2, 0.2)), 0.1, 10.0),
        "whole_shifts": draw_whole_shifts(jax.random.fold_in(splits[5], 71), 0),
    }


SEED = 1.0
HEAT_OF_BOILING = 5000.0


def evaporation_group(thermal_kelvins):
    base_values = jnp.power(10.0, jnp.arange(BINS, dtype=jnp.float32) - 3.0)
    clausius_multiplier = (298.15 / thermal_kelvins) * jnp.exp(HEAT_OF_BOILING * (1.0 / 298.15 - 1.0 / thermal_kelvins))
    return base_values[:, None, None, None] * clausius_multiplier[None]


def band_factors(diffusive_numbers):
    layers = diffusive_numbers.shape[0] + 1
    nothing = jnp.zeros_like(diffusive_numbers[0])
    lower_band = [nothing] + [diffusive_numbers[layer_index - 1] for layer_index in range(1, layers)]
    upper_band = [diffusive_numbers[layer_index] for layer_index in range(layers - 1)] + [nothing]
    ratios = []
    pivots = []
    previous = nothing
    for layer_index in range(layers):
        pivot = 1.0 + lower_band[layer_index] + upper_band[layer_index] - lower_band[layer_index] * previous
        previous = upper_band[layer_index] / pivot
        ratios.append(previous)
        pivots.append(pivot)
    return lower_band, ratios, pivots


def column_solve(right_side, lower_band, ratios, pivots):
    layers = len(pivots)
    partial_value = []
    previous = jnp.zeros_like(right_side[..., 0, :, :])
    for layer_index in range(layers):
        previous = (right_side[..., layer_index, :, :] + lower_band[layer_index] * previous) / pivots[layer_index]
        partial_value.append(previous)
    result = [None] * layers
    following = partial_value[-1]
    result[-1] = following
    for layer_index in range(layers - 2, -1, -1):
        following = partial_value[layer_index] + ratios[layer_index] * following
        result[layer_index] = following
    return jnp.stack(result, axis=-3)


def reference(compound_group_loads, leftover_stepfrac, thermal_kelvins, diffusive_numbers, whole_shifts):
    bin_total = jnp.sum(compound_group_loads, axis=1)
    longitude = jnp.arange(GIRDLE_BOXES, dtype=jnp.int32)
    near_index = (longitude[:, None] - whole_shifts[None, :]) % GIRDLE_BOXES
    far_index = (longitude[:, None] - whole_shifts[None, :] - 1) % GIRDLE_BOXES
    lat_index = jnp.arange(MERIDIAN_LINES, dtype=jnp.int32)[None, :]

    def add_window(distance, window):
        rolled = jnp.roll(bin_total, distance, axis=2)
        return window + jnp.where(distance <= whole_shifts, rolled, 0.0)

    window = lax.fori_loop(1, KMAX + 1, add_window, jnp.zeros_like(bin_total))
    zonal_flux = window + leftover_stepfrac * bin_total[:, :, far_index, lat_index]
    east_frac = jnp.roll(leftover_stepfrac, -1, axis=1)
    advected = (1.0 - east_frac) * compound_group_loads[:, :, :, near_index, lat_index] + leftover_stepfrac * compound_group_loads[:, :, :, far_index, lat_index]
    equilibrium_loading = evaporation_group(thermal_kelvins)
    organic = SEED + jnp.sum(advected, axis=(0, 1))
    for iteration in range(PITERS):
        organic = SEED + jnp.sum(advected / (1.0 + equilibrium_loading / organic), axis=(0, 1))
    condensed = advected / (1.0 + equilibrium_loading / organic)
    lower_band, ratios, pivots = band_factors(diffusive_numbers)
    particle = column_solve(condensed, lower_band, ratios, pivots)
    return particle, zonal_flux
```

```python
import functools

import jax
import jax.numpy as jnp
from jax import lax
from jax.experimental import pallas as pl
from jax.experimental.pallas import tpu as pltpu
from jax.sharding import PartitionSpec as P

BINS = 9
LEVELS = 4
PITERS = 2
CELLS = 16
ROWS = 128
POLAR = 32
SEED = 1.0
HEAT_OF_BOILING = 5000.0
CHUNKS = (2, 2, 2, 2, 2)
SPARES = ((1, 0), (2, 0), (8, 8))

VMEM = pltpu.VMEM
f32, i32 = jnp.float32, jnp.int32


def from_behind(block, axis, distance):
    devices = range(lax.axis_size(axis))
    route = [((i - distance) % len(devices), i) for i in devices]
    return lax.ppermute(block, axis, route)


def along_lanes(values, index):
    return jnp.take_along_axis(values, index, axis=1, mode="promise_in_bounds")


def along_cells(values, index):
    return jnp.take_along_axis(values, index, axis=0, mode="promise_in_bounds")


def vreg_iota(dim):
    return lax.broadcasted_iota(i32, (8, ROWS), dim)


def padded(rows):
    return -(-rows // 8) * 8


def packing(needed):
    ones = jnp.where(needed, 1.0, 0.0).astype(jnp.bfloat16)
    row = lax.broadcasted_iota(i32, (ROWS, ROWS), 0)
    lane = lax.broadcasted_iota(i32, (ROWS, ROWS), 1)
    upto = jnp.where(row <= lane, 1.0, 0.0).astype(jnp.bfloat16)
    ranked = jnp.dot(ones, upto, preferred_element_type=f32).astype(i32)
    count = jnp.sum(jnp.where(needed, 1, 0), axis=1, keepdims=True)
    offsets, running = [], jnp.zeros((1, 1), i32)
    for cell in range(CELLS):
        offsets.append(running)
        running = running + count[cell : cell + 1]
    ends = offsets[1:] + [running]
    offset = jnp.concatenate(offsets, axis=0)
    lanes = lax.broadcasted_iota(i32, (CELLS, ROWS), 1)
    heights = lax.broadcasted_iota(i32, (CELLS, ROWS), 0)
    flat = offset + ranked - 1
    unpack_lane = flat & 127
    unpack_row = (offset >> 7) + jnp.where(lanes < (offset & 127), 1, 0)
    place = heights * ROWS + lanes
    pack_row = jnp.zeros((CELLS, ROWS), i32)
    for cell in range(CELLS):
        pack_row = pack_row + jnp.where(place >= ends[cell], 1, 0)
    pack_row = jnp.minimum(pack_row, CELLS - 1)
    wanted = (lanes - offset) & 127
    halves = []
    for half in range(2):
        at = slice(8 * half, 8 * half + 8)
        position = jnp.zeros((8, ROWS), i32)
        for step in (64, 32, 16, 8, 4, 2, 1):
            probe = along_lanes(ranked[at], position + (step - 1))
            position = jnp.where(probe <= wanted[at], position + step, position)
        halves.append(position)
    return jnp.concatenate(halves, axis=0), pack_row, unpack_row, unpack_lane


def tables_kernel(shifts_ref, near_ref, polar_ref):
    shifts = jnp.broadcast_to(shifts_ref[...], (CELLS, ROWS))
    cell = lax.broadcasted_iota(i32, (CELLS, ROWS), 0)
    needed = jnp.where(
        shifts < CELLS, jnp.where(cell <= shifts, 1, 0),
        jnp.where((cell == 0) | (cell > shifts - CELLS), 1, 0),
    ) > 0
    for at, table in enumerate(packing(needed)):
        near_ref[CELLS * at : CELLS * at + CELLS, :] = table
    within = vreg_iota(1) & (POLAR - 1)
    folded = along_lanes(shifts[:8], within)
    folded = jnp.concatenate([folded, folded], axis=0)
    needed = cell <= folded - CELLS
    pack_lane, pack_row, unpack_row, unpack_lane = packing(needed)
    polar_ref[0:16, :] = pack_lane
    polar_ref[16:32, :] = pack_row
    polar_ref[32:48, :] = unpack_row
    for level in range(LEVELS):
        for half in range(2):
            start = 48 + CELLS * level + 8 * half
            polar_ref[start : start + 8, :] = along_lanes(
                unpack_lane[8 * half : 8 * half + 8], within + POLAR * level
            )


def make_tables(shifts):
    return pl.pallas_call(
        tables_kernel,
        out_shape=(
            jax.ShapeDtypeStruct((4 * CELLS, ROWS), i32),
            jax.ShapeDtypeStruct((3 * CELLS + LEVELS * CELLS, ROWS), i32),
        ),
        name="tables",
    )(shifts)


def turning(shifts):
    back = vreg_iota(0) - shifts - 1
    return back & 7, (back & 15) >= 8


def turned(low, high, turn):
    index, swap = turn
    low, high = along_cells(low, index), along_cells(high, index)
    return jnp.where(swap, high, low), jnp.where(swap, low, high)


def far_masks(shifts):
    cell = vreg_iota(0)
    masks = []
    for half in range(2):
        at = cell + 8 * half
        polar = at <= shifts - CELLS
        behind = at <= shifts
        masks.append((behind, polar))
    return masks


def near_of(far, first):
    last = vreg_iota(0) == 7
    rolled = [pltpu.roll(half, 7, 0) for half in (far[0], far[1], first)]
    return (
        jnp.where(last, rolled[1], rolled[0]),
        jnp.where(last, rolled[2], rolled[1]),
    )


def species_kernel(me_ref, shifts_ref, loads_ref, part0, part1, part2, part3, total_ref):
    parts = (part0, part1, part2, part3)
    shifts = jnp.broadcast_to(shifts_ref[...], (8, ROWS))
    turn = turning(shifts)
    species = loads_ref.shape[0]
    for which, part in enumerate(parts):
        level = (me_ref[0] + which) % LEVELS
        masses = [None] * species
        for b in range(BINS):
            low = high = None
            for s in range(species):
                a, c = loads_ref[s, b, level, 0:8, :], loads_ref[s, b, level, 8:16, :]
                low = a if low is None else low + a
                high = c if high is None else high + c
                both = a + c
                masses[s] = both if b == 0 else masses[s] + both
            low, high = turned(low, high, turn)
            part[b, 0:8, :] = low
            part[b, 8:16, :] = high
        for s in range(species):
            total_ref[s, pl.ds(level, 1), :] = jnp.sum(masses[s], axis=0, keepdims=True)


def species_sums(me, shifts, loads):
    species = loads.shape[0]
    block = jax.ShapeDtypeStruct((BINS, CELLS, ROWS), f32)
    return pl.pallas_call(
        species_kernel,
        out_shape=(block,) * 4 + (jax.ShapeDtypeStruct((species, LEVELS, ROWS), f32),),
        in_specs=[
            pl.BlockSpec(memory_space=pltpu.SMEM),
            pl.BlockSpec(memory_space=VMEM),
            pl.BlockSpec(memory_space=VMEM),
        ],
        out_specs=(pl.BlockSpec(memory_space=VMEM),) * 5,
        name="species_sums",
        cost_estimate=pl.CostEstimate(flops=2_000_000, bytes_accessed=3_300_000, transcendentals=0),
    )(me, shifts, loads)


def organic_kernel(
    shifts_ref, own_ref, behind_ref, polar_ref, frac_ref, east_ref, temp_ref, out_ref
):
    shifts = jnp.broadcast_to(shifts_ref[...], (8, ROWS))
    masks = far_masks(shifts)
    is_polar = shifts >= CELLS
    frac = (frac_ref[0, 0:8, :], frac_ref[0, 8:16, :])
    east = jnp.broadcast_to(east_ref[0], (8, ROWS))
    rest = tuple(1.0 - v for v in near_of(frac, east))
    advected = []
    for b in range(BINS):
        far = []
        for half in range(2):
            at = slice(8 * half, 8 * half + 8)
            behind, polar = masks[half]
            far.append(
                jnp.where(
                    polar, polar_ref[b, at, :],
                    jnp.where(behind, behind_ref[b, at, :], own_ref[b, at, :]),
                )
            )
        first = jnp.where(is_polar, behind_ref[b, 0:8, :], own_ref[b, 0:8, :])
        near = near_of(far, first)
        advected.append([rest[h] * near[h] + frac[h] * far[h] for h in range(2)])
    for half in range(2):
        at = slice(8 * half, 8 * half + 8)
        temp = temp_ref[0, at, :]
        base = (298.15 / temp) * jnp.exp(HEAT_OF_BOILING * (1.0 / 298.15 - 1.0 / temp))
        organic = SEED + sum(advected[b][half] for b in range(BINS))
        for _ in range(PITERS):
            ratio = base / organic
            organic = SEED + sum(
                advected[b][half] / (1.0 + 10.0 ** (b - 3) * ratio) for b in range(BINS)
            )
        out_ref[8 * half : 8 * half + 8, :] = rest[half]
        out_ref[16 + 8 * half : 24 + 8 * half, :] = frac[half]
        out_ref[32 + 8 * half : 40 + 8 * half, :] = base / organic


def organic_of(shifts, own, behind, polar, frac, east, temp):
    return pl.pallas_call(
        organic_kernel,
        out_shape=jax.ShapeDtypeStruct((3 * CELLS, ROWS), f32),
        name="organic",
        cost_estimate=pl.CostEstimate(flops=500_000, bytes_accessed=300_000, transcendentals=2048),
    )(shifts, own, behind, polar, frac, east, temp)


def pack_kernel(spare, polar_spare, shifts_ref, near_ref, polar_ref, loads_ref, ahead_ref, beyond_ref):
    shifts = jnp.broadcast_to(shifts_ref[...], (8, ROWS))
    turn = turning(shifts)

    def table(ref, which, half):
        start = CELLS * which + 8 * half
        return ref[start : start + 8, :]

    def packer(ref, extra):
        lanes = (table(ref, 0, 0), table(ref, 0, 1))
        rows = table(ref, 1, 0)
        later = jnp.maximum(table(ref, 1, 1) - 8, 0)
        early, rows = rows < 8, rows & 7

        def pack(low, high):
            low, high = along_lanes(low, lanes[0]), along_lanes(high, lanes[1])
            main = jnp.where(early, along_cells(low, rows), along_cells(high, rows))
            return main, along_cells(high, later) if extra else None

        return pack

    pack_near = packer(near_ref, spare)
    pack_polar = packer(polar_ref, polar_spare)
    lane = vreg_iota(1)
    for b in range(BINS):
        folded = None
        for level in range(LEVELS):
            low, high = turned(
                loads_ref[0, b, level, 0:8, :], loads_ref[0, b, level, 8:16, :], turn
            )
            if level == 0:
                folded = [low, high]
            else:
                here = lane >= POLAR * level
                folded = [
                    jnp.where(here, pltpu.roll(half, POLAR * level, 1), before)
                    for half, before in zip((low, high), folded)
                ]
            main, extra = pack_near(low, high)
            plane = b * LEVELS + level
            ahead_ref[0, 8 * plane : 8 * plane + 8, :] = main
            if spare:
                start = 8 * BINS * LEVELS + plane * spare
                ahead_ref[0, start : start + spare, :] = extra[:spare]
        main, extra = pack_polar(*folded)
        beyond_ref[0, 8 * b : 8 * b + 8, :] = main
        if polar_spare:
            start = 8 * BINS + b * polar_spare
            beyond_ref[0, start : start + polar_spare, :] = extra[:polar_spare]


def packed_rows(spare, polar_spare):
    return (
        8 * BINS * LEVELS + padded(BINS * LEVELS * spare),
        8 * BINS + padded(BINS * polar_spare),
    )


def whole_spec(shape):
    return pl.BlockSpec(shape, lambda i: (0,) * len(shape))


def pack(spares, start, count, shifts, near_table, polar_table, loads):
    rows, polar_rows = packed_rows(*spares)
    return pl.pallas_call(
        functools.partial(pack_kernel, *spares),
        grid=(count,),
        out_shape=(
            jax.ShapeDtypeStruct((count, rows, ROWS), f32),
            jax.ShapeDtypeStruct((count, polar_rows, ROWS), f32),
        ),
        in_specs=[
            whole_spec((1, ROWS)),
            whole_spec(near_table.shape),
            whole_spec(polar_table.shape),
            pl.BlockSpec((1, BINS, LEVELS, CELLS, ROWS), lambda i: (i + start, 0, 0, 0, 0)),
        ],
        out_specs=(
            pl.BlockSpec((1, rows, ROWS), lambda i: (i, 0, 0)),
            pl.BlockSpec((1, polar_rows, ROWS), lambda i: (i, 0, 0)),
        ),
        name=f"pack_{start}",
        cost_estimate=pl.CostEstimate(
            flops=500_000 * count, bytes_accessed=500_000 * count, transcendentals=0
        ),
    )(shifts, near_table, polar_table, loads)


def final_kernel(
    spare, polar_spare, first_call,
    me_ref, shifts_ref, near_ref, polar_ref, level0, level1, level2, level3, diff_ref,
    loads_ref, behind_ref, beyond_ref, total_ref, *rest,
):
    particle_ref, flux_ref, near_w, far_w, solve, fracs = rest if first_call else rest[2:]
    shifts = jnp.broadcast_to(shifts_ref[...], (8, ROWS))
    halves = (slice(0, 8), slice(8, 16))

    @pl.when(pl.program_id(0) == 0)
    def _():
        for half, at in enumerate(halves):
            diffusive = [diff_ref[k, at, :] for k in range(LEVELS - 1)]
            nothing = jnp.zeros((8, ROWS), f32)
            lower = [nothing] + diffusive
            upper = diffusive + [nothing]
            previous = nothing
            for k in range(LEVELS):
                pivot = 1.0 + lower[k] + upper[k] - lower[k] * previous
                inverse = 1.0 / pivot
                previous = upper[k] * inverse
                solve[0, k, at, :] = inverse
                solve[1, k, at, :] = lower[k] * inverse
                solve[2, k, at, :] = previous
        for which, level_ref in enumerate((level0, level1, level2, level3)):
            level = (me_ref[0] + LEVELS - which) % LEVELS
            for half, at in enumerate(halves):
                rest_of = level_ref[8 * half : 8 * half + 8, :]
                frac = level_ref[16 + 8 * half : 24 + 8 * half, :]
                ratio = level_ref[32 + 8 * half : 40 + 8 * half, :]
                fracs[level, at, :] = frac
                inverse = solve[0, level, at, :]
                for b in range(BINS):
                    weight = inverse / (1.0 + 10.0 ** (b - 3) * ratio)
                    near_w[b, level, at, :] = rest_of * weight
                    far_w[b, level, at, :] = frac * weight

    turn = turning(shifts)
    masks = far_masks(shifts)
    is_polar = shifts >= CELLS

    def table(ref, which, half):
        start = CELLS * which + 8 * half
        return ref[start : start + 8, :]

    row0, row1 = table(near_ref, 2, 0) & 7, table(near_ref, 2, 1)
    row1_low, row1_late = row1 & 7, row1 >= 8
    lanes = (table(near_ref, 3, 0), table(near_ref, 3, 1))
    prow0, prow1 = table(polar_ref, 2, 0) & 7, table(polar_ref, 2, 1)
    prow1_low, prow1_late = prow1 & 7, prow1 >= 8

    sums = [[None] * 5 for _ in range(LEVELS)]
    for b in range(BINS):
        main = beyond_ref[0, 8 * b : 8 * b + 8, :]
        spread = [along_cells(main, prow0), along_cells(main, prow1_low)]
        if polar_spare:
            start = 8 * BINS + b * polar_spare
            late = along_cells(beyond_ref[0, start : start + 8, :], prow1_low)
            spread[1] = jnp.where(prow1_late, late, spread[1])
        forward = [None] * LEVELS
        previous = None
        for k in range(LEVELS):
            low, high = loads_ref[0, b, k, 0:8, :], loads_ref[0, b, k, 8:16, :]
            own = turned(low, high, turn)
            plane = b * LEVELS + k
            main = behind_ref[0, 8 * plane : 8 * plane + 8, :]
            lines = [along_cells(main, row0), along_cells(main, row1_low)]
            start = 8 * BINS * LEVELS + plane * spare
            if spare == 8:
                late = along_cells(behind_ref[0, start : start + 8, :], row1_low)
                lines[1] = jnp.where(row1_late, late, lines[1])
            else:
                for extra in range(spare):
                    late = jnp.broadcast_to(
                        behind_ref[0, start + extra : start + extra + 1, :], (8, ROWS)
                    )
                    lines[1] = jnp.where(row1 == 8 + extra, late, lines[1])
            far, behind = [], []
            for half in range(2):
                from_one = along_lanes(lines[half], lanes[half])
                from_two = along_lanes(
                    spread[half], polar_ref[48 + CELLS * k + 8 * half : 56 + CELLS * k + 8 * half, :]
                )
                is_behind, is_beyond = masks[half]
                behind.append(from_one)
                far.append(
                    jnp.where(is_beyond, from_two, jnp.where(is_behind, from_one, own[half]))
                )
            first = jnp.where(is_polar, behind[0], own[0])
            near = near_of(far, first)
            terms = (far[0], far[1], first, low, high)
            sums[k] = [t if a is None else a + t for a, t in zip(sums[k], terms)]
            step = []
            for half, at in enumerate(halves):
                value = near_w[b, k, at, :] * near[half] + far_w[b, k, at, :] * far[half]
                if k:
                    value = value + solve[1, k, at, :] * previous[half]
                step.append(value)
            forward[k] = previous = step
        following = forward[LEVELS - 1]
        for half, at in enumerate(halves):
            particle_ref[0, b, LEVELS - 1, at, :] = following[half]
        for k in range(LEVELS - 2, -1, -1):
            following = [
                forward[k][half] + solve[2, k, at, :] * following[half]
                for half, at in enumerate(halves)
            ]
            for half, at in enumerate(halves):
                particle_ref[0, b, k, at, :] = following[half]

    cell = vreg_iota(0)
    within = shifts & (CELLS - 1)
    for k in range(LEVELS):
        far0, far1, first, low, high = sums[k]
        near0, near1 = near_of((far0, far1), first)
        counted = jnp.where((cell >= 1) & (cell <= within), far0, 0.0) + jnp.where(
            cell + 8 <= within, far1, 0.0
        )
        window = jnp.sum(counted, axis=0, keepdims=True)
        window = window + jnp.where(
            shifts_ref[...] >= CELLS, total_ref[0, k : k + 1, :], 0.0
        )
        base = jnp.broadcast_to(window, (8, ROWS))
        for half, (gained, lost, far) in enumerate(((low, near0, far0), (high, near1, far1))):
            change = gained - lost
            running = change
            for step in (1, 2, 4):
                running = running + jnp.where(cell >= step, pltpu.roll(running, step, 0), 0.0)
            at = halves[half]
            flux_ref[0, k, at, :] = base + (running - change) + fracs[k, at, :] * far
            if half == 0:
                base = base + jnp.broadcast_to(running[7:8, :], (8, ROWS))


def final(
    spares, start, count, me, shifts, near_table, polar_table, levels, diffusive, loads, behind,
    beyond, totals, before,
):
    species = loads.shape[0]
    outs = (
        jax.ShapeDtypeStruct((species, BINS, LEVELS, CELLS, ROWS), f32),
        jax.ShapeDtypeStruct((species, LEVELS, CELLS, ROWS), f32),
    )
    fixed = [shifts, near_table, polar_table, *levels, diffusive]
    args = [me, *fixed, loads, behind, beyond, totals]
    in_specs = [pl.BlockSpec(memory_space=pltpu.SMEM)]
    in_specs += [whole_spec(a.shape) for a in fixed]
    in_specs += [
        pl.BlockSpec((1, BINS, LEVELS, CELLS, ROWS), lambda i: (i + start, 0, 0, 0, 0)),
        pl.BlockSpec((1,) + behind.shape[1:], lambda i: (i, 0, 0)),
        pl.BlockSpec((1,) + beyond.shape[1:], lambda i: (i, 0, 0)),
        pl.BlockSpec((1, LEVELS, ROWS), lambda i: (i + start, 0, 0)),
    ]
    aliases = {}
    if before is not None:
        aliases = {len(args): 0, len(args) + 1: 1}
        args += list(before)
        in_specs += [pl.BlockSpec(memory_space=pl.ANY)] * 2
    return pl.pallas_call(
        functools.partial(final_kernel, *spares, before is None),
        grid=(count,),
        out_shape=outs,
        in_specs=in_specs,
        out_specs=(
            pl.BlockSpec((1, BINS, LEVELS, CELLS, ROWS), lambda i: (i + start, 0, 0, 0, 0)),
            pl.BlockSpec((1, LEVELS, CELLS, ROWS), lambda i: (i + start, 0, 0, 0)),
        ),
        scratch_shapes=[
            VMEM((BINS, LEVELS, CELLS, ROWS), f32),
            VMEM((BINS, LEVELS, CELLS, ROWS), f32),
            VMEM((3, LEVELS, CELLS, ROWS), f32),
            VMEM((LEVELS, CELLS, ROWS), f32),
        ],
        input_output_aliases=aliases,
        name=f"final_{start}",
        cost_estimate=pl.CostEstimate(
            flops=2_000_000 * count, bytes_accessed=900_000 * count, transcendentals=0
        ),
    )(*args)


def pipeline(spares, me, shifts, loads, frac, temp, diffusive):
    near_table, polar_table = make_tables(shifts)
    east = from_behind(frac[:, :1, :], "lon", -1)
    starts = [sum(CHUNKS[:i]) for i in range(len(CHUNKS))]
    *parts, totals = species_sums(me, shifts, loads)
    parts = [parts[0]] + [from_behind(parts[i], "spc", i) for i in range(1, LEVELS)]
    sent = []
    for start, count in zip(starts, CHUNKS):
        ahead, beyond = pack(spares, start, count, shifts, near_table, polar_table, loads)
        sent.append((from_behind(ahead, "lon", 1), from_behind(beyond, "lon", 2)))
    totals = from_behind(totals, "lon", 1)
    own = parts[0] + parts[1] + parts[2] + parts[3]
    level = organic_of(
        shifts, own, from_behind(own, "lon", 1), from_behind(own, "lon", 2), frac, east, temp
    )
    levels = [level] + [from_behind(level, "spc", i) for i in range(1, LEVELS)]
    outs = None
    for start, count, (behind, beyond) in zip(starts, CHUNKS, sent):
        outs = final(
            spares, start, count, me, shifts, near_table, polar_table, levels, diffusive, loads,
            behind, beyond, totals, outs,
        )
    return tuple(outs)


def per_device(loads, frac, temp, diffusive, whole_shifts):
    me = lax.axis_index("spc").astype(i32).reshape(1)
    shifts = whole_shifts.reshape(1, ROWS)
    near = jnp.sum(jnp.where(whole_shifts < CELLS, whole_shifts + 1, 2 * CELLS - whole_shifts))
    polar = LEVELS * jnp.sum(jnp.maximum(whole_shifts - (CELLS - 1), 0))
    which = sum(
        jnp.where((near > ROWS * (8 + a)) | (polar > ROWS * (8 + c)), 1, 0)
        for a, c in SPARES[:-1]
    )
    branches = [functools.partial(pipeline, spares) for spares in SPARES]
    return lax.switch(which, branches, me, shifts, loads, frac, temp, diffusive)


def solution(mesh):
    placed = (
        P("spc", None, None, "lon", None),
        P("spc", "lon", None),
        P("spc", "lon", None),
        P(None, "lon", None),
        P(),
    )
    return jax.shard_map(
        per_device,
        mesh=mesh,
        in_specs=placed,
        out_specs=(P("spc", None, None, "lon", None), P("spc", None, "lon", None)),
        check_vma=False,
    )
```

```python
import functools

import jax
import jax.numpy as jnp
from jax import lax
from jax.experimental import pallas as pl
from jax.experimental.pallas import tpu as pltpu
from jax.sharding import PartitionSpec as P

BINS = 9
LEVELS = 4
PITERS = 2
CELLS = 16
ROWS = 128
POLAR = 32
SEED = 1.0
HEAT_OF_BOILING = 5000.0
CHUNKS = (2, 3, 3, 2)
SPARES = ((1, 0), (2, 0), (8, 8))

VMEM = pltpu.VMEM
COST = pl.CostEstimate(flops=1, bytes_accessed=1, transcendentals=0)
PARAMS = pltpu.CompilerParams(vmem_limit_bytes=16 * 2**20)
f32, i32 = jnp.float32, jnp.int32


def from_behind(block, axis, distance):
    devices = range(lax.axis_size(axis))
    route = [((i - distance) % len(devices), i) for i in devices]
    return lax.ppermute(block, axis, route)


def swapped(block, mask):
    route = [(i, i ^ mask) for i in range(lax.axis_size("spc"))]
    return lax.ppermute(block, "spc", route)


def any_specs(count):
    return [pl.BlockSpec(memory_space=pl.ANY)] * count


def along_lanes(values, index):
    return jnp.take_along_axis(values, index, axis=1, mode="promise_in_bounds")


def along_cells(values, index):
    return jnp.take_along_axis(values, index, axis=0, mode="promise_in_bounds")


def vreg_iota(dim):
    return lax.broadcasted_iota(i32, (8, ROWS), dim)


def padded(rows):
    return -(-rows // 8) * 8


def packing(needed):
    ones = jnp.where(needed, 1.0, 0.0).astype(jnp.bfloat16)
    row = lax.broadcasted_iota(i32, (ROWS, ROWS), 0)
    lane = lax.broadcasted_iota(i32, (ROWS, ROWS), 1)
    upto = jnp.where(row <= lane, 1.0, 0.0).astype(jnp.bfloat16)
    ranked = jnp.dot(ones, upto, preferred_element_type=f32).astype(i32)
    count = jnp.sum(jnp.where(needed, 1, 0), axis=1, keepdims=True)
    offsets, running = [], jnp.zeros((1, 1), i32)
    for cell in range(CELLS):
        offsets.append(running)
        running = running + count[cell : cell + 1]
    ends = offsets[1:] + [running]
    offset = jnp.concatenate(offsets, axis=0)
    lanes = lax.broadcasted_iota(i32, (CELLS, ROWS), 1)
    heights = lax.broadcasted_iota(i32, (CELLS, ROWS), 0)
    flat = offset + ranked - 1
    unpack_lane = flat & 127
    unpack_row = (offset >> 7) + jnp.where(lanes < (offset & 127), 1, 0)
    place = heights * ROWS + lanes
    pack_row = jnp.zeros((CELLS, ROWS), i32)
    for cell in range(CELLS):
        pack_row = pack_row + jnp.where(place >= ends[cell], 1, 0)
    pack_row = jnp.minimum(pack_row, CELLS - 1)
    wanted = (lanes - offset) & 127
    halves = []
    for half in range(2):
        at = slice(8 * half, 8 * half + 8)
        position = jnp.zeros((8, ROWS), i32)
        for step in (64, 32, 16, 8, 4, 2, 1):
            probe = along_lanes(ranked[at], position + (step - 1))
            position = jnp.where(probe <= wanted[at], position + step, position)
        halves.append(position)
    return (jnp.concatenate(halves, axis=0), pack_row, unpack_row, unpack_lane), running


def tables_kernel(shifts_ref, near_ref, polar_ref, which_ref):
    shifts = jnp.broadcast_to(shifts_ref[...], (CELLS, ROWS))
    cell = lax.broadcasted_iota(i32, (CELLS, ROWS), 0)
    needed = jnp.where(
        shifts < CELLS, jnp.where(cell <= shifts, 1, 0),
        jnp.where((cell == 0) | (cell > shifts - CELLS), 1, 0),
    ) > 0
    made, near_cells = packing(needed)
    for at, table in enumerate(made):
        near_ref[CELLS * at : CELLS * at + CELLS, :] = table
    within = vreg_iota(1) & (POLAR - 1)
    folded = along_lanes(shifts[:8], within)
    folded = jnp.concatenate([folded, folded], axis=0)
    needed = cell <= folded - CELLS
    (pack_lane, pack_row, unpack_row, unpack_lane), polar_cells = packing(needed)
    near_cells, polar_cells = jnp.sum(near_cells), jnp.sum(polar_cells)
    which_ref[0] = sum(
        jnp.where((near_cells > ROWS * (8 + a)) | (polar_cells > ROWS * (8 + c)), 1, 0)
        for a, c in SPARES[:-1]
    )
    polar_ref[0:16, :] = pack_lane
    polar_ref[16:32, :] = pack_row
    polar_ref[32:48, :] = unpack_row
    for level in range(LEVELS):
        for half in range(2):
            start = 48 + CELLS * level + 8 * half
            polar_ref[start : start + 8, :] = along_lanes(
                unpack_lane[8 * half : 8 * half + 8], within + POLAR * level
            )


def make_tables(shifts):
    return pl.pallas_call(
        tables_kernel,
        out_shape=(
            jax.ShapeDtypeStruct((4 * CELLS, ROWS), i32),
            jax.ShapeDtypeStruct((3 * CELLS + LEVELS * CELLS, ROWS), i32),
            jax.ShapeDtypeStruct((1,), i32),
        ),
        out_specs=(
            pl.BlockSpec(memory_space=VMEM),
            pl.BlockSpec(memory_space=VMEM),
            pl.BlockSpec(memory_space=pltpu.SMEM),
        ),
        name="tables",
        compiler_params=PARAMS,
    )(shifts)


def turning(shifts):
    back = vreg_iota(0) - shifts - 1
    return back & 7, (back & 15) >= 8


def turned(low, high, turn):
    index, swap = turn
    low, high = along_cells(low, index), along_cells(high, index)
    return jnp.where(swap, high, low), jnp.where(swap, low, high)


def far_masks(shifts):
    cell = vreg_iota(0)
    masks = []
    for half in range(2):
        at = cell + 8 * half
        polar = at <= shifts - CELLS
        behind = at <= shifts
        masks.append((behind, polar))
    return masks


def near_of(far, first):
    last = vreg_iota(0) == 7
    rolled = [pltpu.roll(half, 7, 0) for half in (far[0], far[1], first)]
    return (
        jnp.where(last, rolled[1], rolled[0]),
        jnp.where(last, rolled[2], rolled[1]),
    )


def table(ref, which, half):
    begin = CELLS * which + 8 * half
    return ref[begin : begin + 8, :]


def packer(table_ref, spare):
    lanes = (table(table_ref, 0, 0), table(table_ref, 0, 1))
    rows = table(table_ref, 1, 0)
    later = jnp.maximum(table(table_ref, 1, 1) - 8, 0)
    early, rows = rows < 8, rows & 7

    def pack_plane(low, high):
        low, high = along_lanes(low, lanes[0]), along_lanes(high, lanes[1])
        main = jnp.where(early, along_cells(low, rows), along_cells(high, rows))
        return main, along_cells(high, later) if spare else None

    return pack_plane


def folded_in(before, plane, place):
    if before is None:
        return list(plane)
    here = vreg_iota(1) >= POLAR * place
    return [
        jnp.where(here, pltpu.roll(half, POLAR * place, 1), old)
        for half, old in zip(plane, before)
    ]


def put_extra(ref, lead, begin, spare, extra):
    if spare == 8:
        ref[(*lead, pl.ds(pl.multiple_of(begin, 8), 8), slice(None))] = extra
    else:
        for row in range(spare):
            ref[(*lead, pl.ds(begin + row, 1), slice(None))] = extra[row : row + 1]


def get_extra(ref, lead, begin, spare):
    if spare == 8:
        return [ref[(*lead, pl.ds(pl.multiple_of(begin, 8), 8), slice(None))]]
    return [
        jnp.broadcast_to(ref[(*lead, pl.ds(begin + row, 1), slice(None))], (8, ROWS))
        for row in range(spare)
    ]


def liner(table_ref, spare):
    row0, row1 = table(table_ref, 2, 0) & 7, table(table_ref, 2, 1)
    low_row, late_row = row1 & 7, row1 >= 8

    def lines(main, extra):
        low, high = along_cells(main, row0), along_cells(main, low_row)
        if spare == 8:
            high = jnp.where(late_row, along_cells(extra[0], low_row), high)
        else:
            for row, late in enumerate(extra):
                high = jnp.where(row1 == 8 + row, late, high)
        return [low, high]

    return lines


def far_of(own, behind, beyond, masks):
    return [
        jnp.where(masks[h][1], beyond[h], jnp.where(masks[h][0], behind[h], own[h]))
        for h in range(2)
    ]


def species_kernel(me_ref, shifts_ref, loads_ref, after_ref, keep_ref, send_ref):
    del after_ref
    shifts = jnp.broadcast_to(shifts_ref[...], (8, ROWS))
    turn = turning(shifts)
    species = loads_ref.shape[0]

    def body(b, carry):
        for away, (part, at) in enumerate(((keep_ref, 0), (send_ref, 0), (keep_ref, 1), (send_ref, 1))):
            level = jnp.bitwise_xor(me_ref[0], away)
            low = sum(loads_ref[s, b, level, 0:8, :] for s in range(1, species))
            high = sum(loads_ref[s, b, level, 8:16, :] for s in range(1, species))
            low = low + loads_ref[0, b, level, 0:8, :]
            high = high + loads_ref[0, b, level, 8:16, :]
            low, high = turned(low, high, turn)
            part[at, b, 0:8, :] = low
            part[at, b, 8:16, :] = high
        return carry

    lax.fori_loop(0, BINS, body, 0)


def species_sums(me, shifts, loads, after):
    return pl.pallas_call(
        species_kernel,
        out_shape=(jax.ShapeDtypeStruct((2, BINS, CELLS, ROWS), f32),) * 2,
        in_specs=[
            pl.BlockSpec(memory_space=pltpu.SMEM),
            pl.BlockSpec(memory_space=VMEM),
            pl.BlockSpec(memory_space=VMEM),
        ]
        + any_specs(1),
        out_specs=(pl.BlockSpec(memory_space=VMEM),) * 2,
        name="species_sums",
        compiler_params=PARAMS,
        cost_estimate=COST,
    )(me, shifts, loads, after)


PLANES = 2 * BINS
SUMS = PLANES * CELLS
FOLDS = -(-PLANES // LEVELS)


def chip_kernel(keep_ref, got_ref, frac_ref, east_ref, temp_ref, out_ref):
    for at in range(2):
        for b in range(BINS):
            begin = CELLS * (BINS * at + b)
            out_ref[begin : begin + CELLS, :] = keep_ref[at, b] + got_ref[at, b]
    frac = (frac_ref[0, 0:8, :], frac_ref[0, 8:16, :])
    east = near_of(frac, jnp.broadcast_to(east_ref[0], (8, ROWS)))
    for half in range(2):
        begin = SUMS + 8 * half
        out_ref[begin : begin + 8, :] = 1.0 - east[half]
        out_ref[begin + 16 : begin + 24, :] = frac[half]
        out_ref[begin + 32 : begin + 40, :] = temp_ref[0, 8 * half : 8 * half + 8, :]


def chip_sums(keep, got, frac, east, temp):
    return pl.pallas_call(
        chip_kernel,
        out_shape=jax.ShapeDtypeStruct((SUMS + 3 * CELLS, ROWS), f32),
        in_specs=[pl.BlockSpec(memory_space=VMEM)] * 5,
        out_specs=pl.BlockSpec(memory_space=VMEM),
        name="chip_sums",
        compiler_params=PARAMS,
        cost_estimate=COST,
    )(keep, got, frac, east, temp)


def all_kernel(spare, polar_spare, near_ref, polar_ref, mine_ref, other_ref, own_ref, ahead_ref, beyond_ref):
    pack_near, pack_polar = packer(near_ref, spare), packer(polar_ref, polar_spare)
    folded = None
    for plane in range(PLANES):
        begin = CELLS * plane
        across = CELLS * ((plane + BINS) % PLANES)
        low = mine_ref[begin : begin + 8, :] + other_ref[across : across + 8, :]
        high = mine_ref[begin + 8 : begin + 16, :] + other_ref[across + 8 : across + 16, :]
        own_ref[begin : begin + 8, :] = low
        own_ref[begin + 8 : begin + 16, :] = high
        main, extra = pack_near(low, high)
        ahead_ref[8 * plane : 8 * plane + 8, :] = main
        put_extra(ahead_ref, (), 8 * PLANES + plane * spare, spare, extra)
        place = plane % LEVELS
        folded = folded_in(folded if place else None, (low, high), place)
        if place == LEVELS - 1 or plane == PLANES - 1:
            fold = plane // LEVELS
            main, extra = pack_polar(*folded)
            beyond_ref[8 * fold : 8 * fold + 8, :] = main
            put_extra(beyond_ref, (), 8 * FOLDS + fold * polar_spare, polar_spare, extra)


def all_sums(spares, near_table, polar_table, mine, other):
    spare, polar_spare = spares
    return pl.pallas_call(
        functools.partial(all_kernel, spare, polar_spare),
        out_shape=(
            jax.ShapeDtypeStruct((SUMS, ROWS), f32),
            jax.ShapeDtypeStruct((padded((8 + spare) * PLANES), ROWS), f32),
            jax.ShapeDtypeStruct(((8 + polar_spare) * FOLDS, ROWS), f32),
        ),
        in_specs=[pl.BlockSpec(memory_space=VMEM)] * 4,
        out_specs=(pl.BlockSpec(memory_space=VMEM),) * 3,
        name="all_sums",
        compiler_params=PARAMS,
        cost_estimate=COST,
    )(near_table, polar_table, mine, other)


def organic_kernel(
    spare, polar_spare,
    shifts_ref, near_ref, polar_ref, own_ref, behind_ref, beyond_ref, mine_ref, other_ref, after_ref,
    out_ref,
):
    del after_ref
    shifts = jnp.broadcast_to(shifts_ref[...], (8, ROWS))
    masks = far_masks(shifts)
    is_polar = shifts >= CELLS
    near_lines, polar_lines = liner(near_ref, spare), liner(polar_ref, polar_spare)
    lanes = (table(near_ref, 3, 0), table(near_ref, 3, 1))
    spread = None
    for at, meta_ref in enumerate((mine_ref, other_ref)):
        meta = [
            [meta_ref[SUMS + 16 * n + 8 * h : SUMS + 16 * n + 8 * h + 8, :] for h in range(2)]
            for n in range(3)
        ]
        rest, frac, temp = meta
        advected = []
        for b in range(BINS):
            plane = BINS * at + b
            begin, fold, place = CELLS * plane, plane // LEVELS, plane % LEVELS
            own = (own_ref[begin : begin + 8, :], own_ref[begin + 8 : begin + 16, :])
            if place == 0:
                spread = polar_lines(
                    beyond_ref[8 * fold : 8 * fold + 8, :],
                    get_extra(beyond_ref, (), 8 * FOLDS + fold * polar_spare, polar_spare),
                )
            lines = near_lines(
                behind_ref[8 * plane : 8 * plane + 8, :],
                get_extra(behind_ref, (), 8 * PLANES + plane * spare, spare),
            )
            behind = [along_lanes(lines[h], lanes[h]) for h in range(2)]
            beyond = [along_lanes(spread[h], table(polar_ref, 3 + place, h)) for h in range(2)]
            far = far_of(own, behind, beyond, masks)
            near = near_of(far, jnp.where(is_polar, behind[0], own[0]))
            advected.append([rest[h] * near[h] + frac[h] * far[h] for h in range(2)])
        for half in range(2):
            base = (298.15 / temp[half]) * jnp.exp(
                HEAT_OF_BOILING * (1.0 / 298.15 - 1.0 / temp[half])
            )
            organic = SEED + sum(advected[b][half] for b in range(BINS))
            for _ in range(PITERS):
                ratio = base / organic
                organic = SEED + sum(
                    advected[b][half] / (1.0 + 10.0 ** (b - 3) * ratio) for b in range(BINS)
                )
            out_ref[at, 8 * half : 8 * half + 8, :] = rest[half]
            out_ref[at, 16 + 8 * half : 24 + 8 * half, :] = frac[half]
            out_ref[at, 32 + 8 * half : 40 + 8 * half, :] = base / organic


def organic_of(spares, shifts, near_table, polar_table, own, behind, beyond, mine, other, after):
    return pl.pallas_call(
        functools.partial(organic_kernel, *spares),
        out_shape=jax.ShapeDtypeStruct((2, 3 * CELLS, ROWS), f32),
        in_specs=[pl.BlockSpec(memory_space=VMEM)] * 8 + any_specs(1),
        out_specs=pl.BlockSpec(memory_space=VMEM),
        name="organic",
        compiler_params=PARAMS,
        cost_estimate=COST,
    )(shifts, near_table, polar_table, own, behind, beyond, mine, other, after)


def pack_kernel(
    spare, polar_spare, start, shifts_ref, near_ref, polar_ref, loads_ref, *rest
):
    ahead_ref, beyond_ref = rest[-2:]
    shifts = jnp.broadcast_to(shifts_ref[...], (8, ROWS))
    turn = turning(shifts)
    s = pl.program_id(0) + start

    pack_near, pack_polar = packer(near_ref, spare), packer(polar_ref, polar_spare)

    def body(b, totals):
        folded, sums = None, []
        for level in range(LEVELS):
            low, high = turned(
                loads_ref[s, b, level, 0:8, :], loads_ref[s, b, level, 8:16, :], turn
            )
            sums.append(totals[level] + (low + high))
            folded = folded_in(folded, (low, high), level)
            main, extra = pack_near(low, high)
            plane = b * LEVELS + level
            ahead_ref[0, pl.ds(pl.multiple_of(8 * plane, 8), 8), :] = main
            put_extra(ahead_ref, (0,), 8 * BINS * LEVELS + plane * spare, spare, extra)
        main, extra = pack_polar(*folded)
        beyond_ref[0, pl.ds(pl.multiple_of(8 * b, 8), 8), :] = main
        put_extra(beyond_ref, (0,), 8 * BINS + b * polar_spare, polar_spare, extra)
        return tuple(sums)

    totals = lax.fori_loop(0, BINS, body, (jnp.zeros((8, ROWS), f32),) * LEVELS, unroll=3)
    begin = (8 + spare) * BINS * LEVELS
    for level in range(LEVELS):
        ahead_ref[0, begin + level : begin + level + 1, :] = jnp.sum(
            totals[level], axis=0, keepdims=True
        )


def packed_rows(spare, polar_spare):
    return (
        padded((8 + spare) * BINS * LEVELS + LEVELS),
        (8 + polar_spare) * BINS,
    )


def whole_spec(shape):
    return pl.BlockSpec(shape, lambda i: (0,) * len(shape))


def pack(spares, start, count, shifts, near_table, polar_table, loads, after, before):
    rows, polar_rows = packed_rows(*spares)
    species = loads.shape[0]
    args = [shifts, near_table, polar_table, loads, *after]
    in_specs = [pl.BlockSpec(memory_space=VMEM)] * 4 + any_specs(len(after))
    aliases = {}
    if before is not None:
        aliases = {len(args): 1}
        args.append(before)
        in_specs.append(pl.BlockSpec(memory_space=pl.ANY))
    return pl.pallas_call(
        functools.partial(pack_kernel, *spares, start),
        grid=(count,),
        out_shape=(
            jax.ShapeDtypeStruct((count, rows, ROWS), f32),
            jax.ShapeDtypeStruct((species, polar_rows, ROWS), f32),
        ),
        in_specs=in_specs,
        out_specs=(
            pl.BlockSpec((1, rows, ROWS), lambda i: (i, 0, 0)),
            pl.BlockSpec((1, polar_rows, ROWS), lambda i: (i + start, 0, 0)),
        ),
        input_output_aliases=aliases,
        name=f"pack_{start}",
        compiler_params=PARAMS,
        cost_estimate=COST,
    )(*args)


def weights_kernel(me_ref, pair_ref, other_ref, diff_ref, near_w, far_w, solve, fracs):
    for half in range(2):
        at = slice(8 * half, 8 * half + 8)
        diffusive = [diff_ref[k, at, :] for k in range(LEVELS - 1)]
        nothing = jnp.zeros((8, ROWS), f32)
        lower = [nothing] + diffusive
        upper = diffusive + [nothing]
        previous = nothing
        for k in range(LEVELS):
            pivot = 1.0 + lower[k] + upper[k] - lower[k] * previous
            inverse = 1.0 / pivot
            previous = upper[k] * inverse
            solve[0, k, at, :] = inverse
            solve[1, k, at, :] = lower[k] * inverse
            solve[2, k, at, :] = previous
    for away in range(LEVELS):
        level_ref = (pair_ref, other_ref)[away & 1].at[away >> 1]
        level = jnp.bitwise_xor(me_ref[0], away)
        for half in range(2):
            at = slice(8 * half, 8 * half + 8)
            rest_of = level_ref[8 * half : 8 * half + 8, :]
            frac = level_ref[16 + 8 * half : 24 + 8 * half, :]
            ratio = level_ref[32 + 8 * half : 40 + 8 * half, :]
            fracs[level, at, :] = frac
            inverse = solve[0, level, at, :]
            near_top, far_top = rest_of * inverse, frac * inverse
            for b in range(BINS):
                weight = 1.0 / (1.0 + 10.0 ** (b - 3) * ratio)
                near_w[b, level, at, :] = near_top * weight
                far_w[b, level, at, :] = far_top * weight


def weights_of(me, pair, other, diffusive):
    block = (LEVELS, CELLS, ROWS)
    return pl.pallas_call(
        weights_kernel,
        out_shape=tuple(
            jax.ShapeDtypeStruct(shape, f32)
            for shape in ((BINS,) + block, (BINS,) + block, (3,) + block, block)
        ),
        in_specs=[pl.BlockSpec(memory_space=pltpu.SMEM)] + [pl.BlockSpec(memory_space=VMEM)] * 3,
        out_specs=(pl.BlockSpec(memory_space=VMEM),) * 4,
        name="weights",
        compiler_params=PARAMS,
        cost_estimate=COST,
    )(me, pair, other, diffusive)


def final_kernel(
    spare, polar_spare, start,
    shifts_ref, near_ref, polar_ref, near_w, far_w, solve, fracs, loads_ref, behind_ref, beyond_ref,
    *rest,
):
    particle_ref, flux_ref = rest[-2:]
    shifts = jnp.broadcast_to(shifts_ref[...], (8, ROWS))
    halves = (slice(0, 8), slice(8, 16))
    turn = turning(shifts)
    masks = far_masks(shifts)
    is_polar = shifts >= CELLS
    i = pl.program_id(0)
    s = i + start

    near_lines, polar_lines = liner(near_ref, spare), liner(polar_ref, polar_spare)
    lanes = (table(near_ref, 3, 0), table(near_ref, 3, 1))

    def body(b, carry):
        spread = polar_lines(
            beyond_ref[s, pl.ds(pl.multiple_of(8 * b, 8), 8), :],
            get_extra(beyond_ref, (s,), 8 * BINS + b * polar_spare, polar_spare),
        )
        forward = [None] * LEVELS
        previous = None
        sums = []
        for k in range(LEVELS):
            low, high = loads_ref[s, b, k, 0:8, :], loads_ref[s, b, k, 8:16, :]
            own = turned(low, high, turn)
            plane = b * LEVELS + k
            lines = near_lines(
                behind_ref[i, pl.ds(pl.multiple_of(8 * plane, 8), 8), :],
                get_extra(behind_ref, (i,), 8 * BINS * LEVELS + plane * spare, spare),
            )
            behind = [along_lanes(lines[h], lanes[h]) for h in range(2)]
            beyond = [along_lanes(spread[h], table(polar_ref, 3 + k, h)) for h in range(2)]
            far = far_of(own, behind, beyond, masks)
            first = jnp.where(is_polar, behind[0], own[0])
            near = near_of(far, first)
            terms = (far[0], far[1], first, low, high)
            sums.append(tuple(a + t for a, t in zip(carry[k], terms)))
            step = []
            for half, at in enumerate(halves):
                value = near_w[b, k, at, :] * near[half] + far_w[b, k, at, :] * far[half]
                if k:
                    value = value + solve[1, k, at, :] * previous[half]
                step.append(value)
            forward[k] = previous = step
        following = forward[LEVELS - 1]
        for half, at in enumerate(halves):
            particle_ref[0, b, LEVELS - 1, at, :] = following[half]
        for k in range(LEVELS - 2, -1, -1):
            following = [
                forward[k][half] + solve[2, k, at, :] * following[half]
                for half, at in enumerate(halves)
            ]
            for half, at in enumerate(halves):
                particle_ref[0, b, k, at, :] = following[half]
        return tuple(sums)

    zero = jnp.zeros((8, ROWS), f32)
    sums = lax.fori_loop(0, BINS, body, ((zero,) * 5,) * LEVELS, unroll=3)
    cell = vreg_iota(0)
    within = shifts & (CELLS - 1)
    for k in range(LEVELS):
        far0, far1, first, low, high = sums[k]
        near0, near1 = near_of((far0, far1), first)
        counted = jnp.where((cell >= 1) & (cell <= within), far0, 0.0) + jnp.where(
            cell + 8 <= within, far1, 0.0
        )
        window = jnp.sum(counted, axis=0, keepdims=True)
        begin = (8 + spare) * BINS * LEVELS + k
        window = window + jnp.where(
            shifts_ref[...] >= CELLS, behind_ref[i, begin : begin + 1, :], 0.0
        )
        base = jnp.broadcast_to(window, (8, ROWS))
        for half, (gained, lost, far) in enumerate(((low, near0, far0), (high, near1, far1))):
            change = gained - lost
            running = change
            for step in (1, 2, 4):
                running = running + jnp.where(cell >= step, pltpu.roll(running, step, 0), 0.0)
            at = halves[half]
            flux_ref[0, k, at, :] = base + (running - change) + fracs[k, at, :] * far
            if half == 0:
                base = base + jnp.broadcast_to(running[7:8, :], (8, ROWS))


def final(
    spares, start, count, shifts, near_table, polar_table, weights, loads, behind, beyond, before
):
    species = loads.shape[0]
    outs = (
        jax.ShapeDtypeStruct((species, BINS, LEVELS, CELLS, ROWS), f32),
        jax.ShapeDtypeStruct((species, LEVELS, CELLS, ROWS), f32),
    )
    args = [shifts, near_table, polar_table, *weights, loads, behind, beyond]
    in_specs = [pl.BlockSpec(memory_space=VMEM)] * len(args)
    aliases = {}
    if before is not None:
        aliases = {len(args): 0, len(args) + 1: 1}
        args += list(before)
        in_specs += [pl.BlockSpec(memory_space=pl.ANY)] * 2
    return pl.pallas_call(
        functools.partial(final_kernel, *spares, start),
        grid=(count,),
        out_shape=outs,
        in_specs=in_specs,
        out_specs=(
            pl.BlockSpec((1, BINS, LEVELS, CELLS, ROWS), lambda i: (i + start, 0, 0, 0, 0)),
            pl.BlockSpec((1, LEVELS, CELLS, ROWS), lambda i: (i + start, 0, 0, 0)),
        ),
        input_output_aliases=aliases,
        name=f"final_{start}",
        compiler_params=PARAMS,
        cost_estimate=COST,
    )(*args)


def along_meridian(block):
    size = lax.axis_size("lon")
    return lax.ppermute(block, "lon", [(i, (i + 2) % size) for i in range(1, size, 2)])


def crossed(block):
    return lax.ppermute(block, "lon", [(i, i ^ 1) for i in range(lax.axis_size("lon"))])


def pipeline(spares, me, shifts, near_table, polar_table, loads, frac, temp, diffusive):
    tables = (shifts, near_table, polar_table)
    odd = lax.axis_index("lon") % 2 == 1
    starts = [sum(CHUNKS[:i]) for i in range(len(CHUNKS))]
    last = len(CHUNKS) - 1
    east = from_behind(frac[:, :1, :], "lon", -1)
    keep, send = species_sums(me, shifts, loads, near_table)
    got = swapped(send, 1)
    after, beyond, aheads = [keep], None, [None] * len(CHUNKS)
    for at in (0, last, 1, 2):
        aheads[at], beyond = pack(
            spares, starts[at], CHUNKS[at], *tables, loads, after, beyond
        )
        after = [aheads[at]]
    relayed = along_meridian(aheads[last])
    mine = chip_sums(keep, got, frac, east, temp)
    other = swapped(mine, 2)
    aheads[0], _ = lax.optimization_barrier((aheads[0], mine))
    behind = [from_behind(aheads[0], "lon", 1), from_behind(aheads[1], "lon", 1)]
    own, ahead_sums, beyond_sums = all_sums(spares, near_table, polar_table, mine, other)
    sums_behind = from_behind(ahead_sums, "lon", 1)
    sums_beyond = from_behind(beyond_sums, "lon", 2)
    beyond = from_behind(beyond, "lon", 2)
    aheads[2], behind[0] = lax.optimization_barrier((aheads[2], behind[0]))
    behind.append(from_behind(aheads[2], "lon", 1))
    mixed, sums_behind, sums_beyond = lax.optimization_barrier(
        (jnp.where(odd, relayed, aheads[last]), sums_behind, sums_beyond)
    )
    behind.append(crossed(mixed))
    level = organic_of(spares, *tables, own, sums_behind, sums_beyond, mine, other, behind[0])
    weights = weights_of(me, level, swapped(level, 1), diffusive)
    outs = None
    for start, count, block in zip(starts, CHUNKS, behind):
        outs = final(spares, start, count, *tables, weights, loads, block, beyond, outs)
    return tuple(outs)


def per_device(loads, frac, temp, diffusive, whole_shifts):
    me = lax.axis_index("spc").astype(i32).reshape(1)
    shifts = whole_shifts.reshape(1, ROWS)
    near_table, polar_table, which = make_tables(shifts)
    branches = [functools.partial(pipeline, spares) for spares in SPARES]
    return lax.switch(
        which[0], branches, me, shifts, near_table, polar_table, loads, frac, temp, diffusive
    )


def solution(mesh):
    placed = (
        P("spc", None, None, "lon", None),
        P("spc", "lon", None),
        P("spc", "lon", None),
        P(None, "lon", None),
        P(),
    )
    return jax.shard_map(
        per_device,
        mesh=mesh,
        in_specs=placed,
        out_specs=(P("spc", None, None, "lon", None), P("spc", None, "lon", None)),
        check_vma=False,
    )
```

```python
import functools

import jax
import jax.numpy as jnp
from jax import lax
from jax.experimental import pallas as pl
from jax.experimental.pallas import tpu as pltpu
from jax.sharding import PartitionSpec as P

BINS = 9
LEVELS = 4
PITERS = 2
CELLS = 16
ROWS = 128
POLAR = 32
SEED = 1.0
HEAT_OF_BOILING = 5000.0
CHUNKS = (2, 3, 3, 2)
SPARES = ((1, 0), (2, 0), (8, 8))

VMEM = pltpu.VMEM
COST = pl.CostEstimate(flops=1, bytes_accessed=1, transcendentals=0)
PARAMS = pltpu.CompilerParams(vmem_limit_bytes=16 * 2**20)
f32, i32 = jnp.float32, jnp.int32


def from_behind(block, axis, distance):
    devices = range(lax.axis_size(axis))
    route = [((i - distance) % len(devices), i) for i in devices]
    return lax.ppermute(block, axis, route)


def swapped(block, mask):
    route = [(i, i ^ mask) for i in range(lax.axis_size("spc"))]
    return lax.ppermute(block, "spc", route)


def any_specs(count):
    return [pl.BlockSpec(memory_space=pl.ANY)] * count


def along_lanes(values, index):
    return jnp.take_along_axis(values, index, axis=1, mode="promise_in_bounds")


def along_cells(values, index):
    return jnp.take_along_axis(values, index, axis=0, mode="promise_in_bounds")


def vreg_iota(dim):
    return lax.broadcasted_iota(i32, (8, ROWS), dim)


def padded(rows):
    return -(-rows // 8) * 8


def packing(needed):
    ones = jnp.where(needed, 1.0, 0.0).astype(jnp.bfloat16)
    row = lax.broadcasted_iota(i32, (ROWS, ROWS), 0)
    lane = lax.broadcasted_iota(i32, (ROWS, ROWS), 1)
    upto = jnp.where(row <= lane, 1.0, 0.0).astype(jnp.bfloat16)
    ranked = jnp.dot(ones, upto, preferred_element_type=f32).astype(i32)
    count = jnp.sum(jnp.where(needed, 1, 0), axis=1, keepdims=True)
    offsets, running = [], jnp.zeros((1, 1), i32)
    for cell in range(CELLS):
        offsets.append(running)
        running = running + count[cell : cell + 1]
    ends = offsets[1:] + [running]
    offset = jnp.concatenate(offsets, axis=0)
    lanes = lax.broadcasted_iota(i32, (CELLS, ROWS), 1)
    heights = lax.broadcasted_iota(i32, (CELLS, ROWS), 0)
    flat = offset + ranked - 1
    unpack_lane = flat & 127
    unpack_row = (offset >> 7) + jnp.where(lanes < (offset & 127), 1, 0)
    place = heights * ROWS + lanes
    pack_row = jnp.zeros((CELLS, ROWS), i32)
    for cell in range(CELLS):
        pack_row = pack_row + jnp.where(place >= ends[cell], 1, 0)
    pack_row = jnp.minimum(pack_row, CELLS - 1)
    wanted = (lanes - offset) & 127
    halves = []
    for half in range(2):
        at = slice(8 * half, 8 * half + 8)
        position = jnp.zeros((8, ROWS), i32)
        for step in (64, 32, 16, 8, 4, 2, 1):
            probe = along_lanes(ranked[at], position + (step - 1))
            position = jnp.where(probe <= wanted[at], position + step, position)
        halves.append(position)
    return (jnp.concatenate(halves, axis=0), pack_row, unpack_row, unpack_lane), running


def tables_kernel(shifts_ref, near_ref, polar_ref, which_ref):
    shifts = jnp.broadcast_to(shifts_ref[...], (CELLS, ROWS))
    cell = lax.broadcasted_iota(i32, (CELLS, ROWS), 0)
    needed = jnp.where(
        shifts < CELLS, jnp.where(cell <= shifts, 1, 0),
        jnp.where((cell == 0) | (cell > shifts - CELLS), 1, 0),
    ) > 0
    made, near_cells = packing(needed)
    for at, table in enumerate(made):
        near_ref[CELLS * at : CELLS * at + CELLS, :] = table
    within = vreg_iota(1) & (POLAR - 1)
    folded = along_lanes(shifts[:8], within)
    folded = jnp.concatenate([folded, folded], axis=0)
    needed = cell <= folded - CELLS
    (pack_lane, pack_row, unpack_row, unpack_lane), polar_cells = packing(needed)
    near_cells, polar_cells = jnp.sum(near_cells), jnp.sum(polar_cells)
    which_ref[0] = sum(
        jnp.where((near_cells > ROWS * (8 + a)) | (polar_cells > ROWS * (8 + c)), 1, 0)
        for a, c in SPARES[:-1]
    )
    polar_ref[0:16, :] = pack_lane
    polar_ref[16:32, :] = pack_row
    polar_ref[32:48, :] = unpack_row
    for level in range(LEVELS):
        for half in range(2):
            start = 48 + CELLS * level + 8 * half
            polar_ref[start : start + 8, :] = along_lanes(
                unpack_lane[8 * half : 8 * half + 8], within + POLAR * level
            )


def make_tables(shifts):
    return pl.pallas_call(
        tables_kernel,
        out_shape=(
            jax.ShapeDtypeStruct((4 * CELLS, ROWS), i32),
            jax.ShapeDtypeStruct((3 * CELLS + LEVELS * CELLS, ROWS), i32),
            jax.ShapeDtypeStruct((1,), i32),
        ),
        out_specs=(
            pl.BlockSpec(memory_space=VMEM),
            pl.BlockSpec(memory_space=VMEM),
            pl.BlockSpec(memory_space=pltpu.SMEM),
        ),
        name="tables",
        compiler_params=PARAMS,
    )(shifts)


def turning(shifts):
    back = vreg_iota(0) - shifts - 1
    return back & 7, (back & 15) >= 8


def turned(low, high, turn):
    index, swap = turn
    low, high = along_cells(low, index), along_cells(high, index)
    return jnp.where(swap, high, low), jnp.where(swap, low, high)


def far_masks(shifts):
    cell = vreg_iota(0)
    masks = []
    for half in range(2):
        at = cell + 8 * half
        polar = at <= shifts - CELLS
        behind = at <= shifts
        masks.append((behind, polar))
    return masks


def near_of(far, first):
    last = vreg_iota(0) == 7
    rolled = [pltpu.roll(half, 7, 0) for half in (far[0], far[1], first)]
    return (
        jnp.where(last, rolled[1], rolled[0]),
        jnp.where(last, rolled[2], rolled[1]),
    )


def table(ref, which, half):
    begin = CELLS * which + 8 * half
    return ref[begin : begin + 8, :]


def packer(table_ref, spare):
    lanes = (table(table_ref, 0, 0), table(table_ref, 0, 1))
    rows = table(table_ref, 1, 0)
    later = jnp.maximum(table(table_ref, 1, 1) - 8, 0)
    early, rows = rows < 8, rows & 7

    def pack_plane(low, high):
        low, high = along_lanes(low, lanes[0]), along_lanes(high, lanes[1])
        main = jnp.where(early, along_cells(low, rows), along_cells(high, rows))
        return main, along_cells(high, later) if spare else None

    return pack_plane


def folded_in(before, plane, place):
    if before is None:
        return list(plane)
    here = vreg_iota(1) >= POLAR * place
    return [
        jnp.where(here, pltpu.roll(half, POLAR * place, 1), old)
        for half, old in zip(plane, before)
    ]


def put_extra(ref, lead, begin, spare, extra):
    if spare == 8:
        ref[(*lead, pl.ds(pl.multiple_of(begin, 8), 8), slice(None))] = extra
    else:
        for row in range(spare):
            ref[(*lead, pl.ds(begin + row, 1), slice(None))] = extra[row : row + 1]


def get_extra(ref, lead, begin, spare):
    if spare == 8:
        return [ref[(*lead, pl.ds(pl.multiple_of(begin, 8), 8), slice(None))]]
    return [
        jnp.broadcast_to(ref[(*lead, pl.ds(begin + row, 1), slice(None))], (8, ROWS))
        for row in range(spare)
    ]


def liner(table_ref, spare):
    row0, row1 = table(table_ref, 2, 0) & 7, table(table_ref, 2, 1)
    low_row, late_row = row1 & 7, row1 >= 8

    def lines(main, extra):
        low, high = along_cells(main, row0), along_cells(main, low_row)
        if spare == 8:
            high = jnp.where(late_row, along_cells(extra[0], low_row), high)
        else:
            for row, late in enumerate(extra):
                high = jnp.where(row1 == 8 + row, late, high)
        return [low, high]

    return lines


def far_of(own, behind, beyond, masks):
    return [
        jnp.where(masks[h][1], beyond[h], jnp.where(masks[h][0], behind[h], own[h]))
        for h in range(2)
    ]


def species_kernel(me_ref, shifts_ref, loads_ref, after_ref, keep_ref, send_ref):
    del after_ref
    shifts = jnp.broadcast_to(shifts_ref[...], (8, ROWS))
    turn = turning(shifts)
    species = loads_ref.shape[0]

    def body(b, carry):
        for away, (part, at) in enumerate(((keep_ref, 0), (send_ref, 0), (keep_ref, 1), (send_ref, 1))):
            level = jnp.bitwise_xor(me_ref[0], away)
            low = sum(loads_ref[s, b, level, 0:8, :] for s in range(1, species))
            high = sum(loads_ref[s, b, level, 8:16, :] for s in range(1, species))
            low = low + loads_ref[0, b, level, 0:8, :]
            high = high + loads_ref[0, b, level, 8:16, :]
            low, high = turned(low, high, turn)
            part[at, b, 0:8, :] = low
            part[at, b, 8:16, :] = high
        return carry

    lax.fori_loop(0, BINS, body, 0)


def species_sums(me, shifts, loads, after):
    return pl.pallas_call(
        species_kernel,
        out_shape=(jax.ShapeDtypeStruct((2, BINS, CELLS, ROWS), f32),) * 2,
        in_specs=[
            pl.BlockSpec(memory_space=pltpu.SMEM),
            pl.BlockSpec(memory_space=VMEM),
            pl.BlockSpec(memory_space=VMEM),
        ]
        + any_specs(1),
        out_specs=(pl.BlockSpec(memory_space=VMEM),) * 2,
        name="species_sums",
        compiler_params=PARAMS,
        cost_estimate=COST,
    )(me, shifts, loads, after)


PLANES = 2 * BINS
SUMS = PLANES * CELLS
FOLDS = -(-PLANES // LEVELS)


def chip_kernel(keep_ref, got_ref, frac_ref, east_ref, temp_ref, out_ref):
    for at in range(2):
        for b in range(BINS):
            begin = CELLS * (BINS * at + b)
            out_ref[begin : begin + CELLS, :] = keep_ref[at, b] + got_ref[at, b]
    frac = (frac_ref[0, 0:8, :], frac_ref[0, 8:16, :])
    east = near_of(frac, jnp.broadcast_to(east_ref[0], (8, ROWS)))
    for half in range(2):
        begin = SUMS + 8 * half
        out_ref[begin : begin + 8, :] = 1.0 - east[half]
        out_ref[begin + 16 : begin + 24, :] = frac[half]
        out_ref[begin + 32 : begin + 40, :] = temp_ref[0, 8 * half : 8 * half + 8, :]


def chip_sums(keep, got, frac, east, temp):
    return pl.pallas_call(
        chip_kernel,
        out_shape=jax.ShapeDtypeStruct((SUMS + 3 * CELLS, ROWS), f32),
        in_specs=[pl.BlockSpec(memory_space=VMEM)] * 5,
        out_specs=pl.BlockSpec(memory_space=VMEM),
        name="chip_sums",
        compiler_params=PARAMS,
        cost_estimate=COST,
    )(keep, got, frac, east, temp)


def all_kernel(spare, polar_spare, near_ref, polar_ref, mine_ref, other_ref, own_ref, ahead_ref, beyond_ref):
    pack_near, pack_polar = packer(near_ref, spare), packer(polar_ref, polar_spare)
    folded = None
    for plane in range(PLANES):
        begin = CELLS * plane
        across = CELLS * ((plane + BINS) % PLANES)
        low = mine_ref[begin : begin + 8, :] + other_ref[across : across + 8, :]
        high = mine_ref[begin + 8 : begin + 16, :] + other_ref[across + 8 : across + 16, :]
        own_ref[begin : begin + 8, :] = low
        own_ref[begin + 8 : begin + 16, :] = high
        main, extra = pack_near(low, high)
        ahead_ref[8 * plane : 8 * plane + 8, :] = main
        put_extra(ahead_ref, (), 8 * PLANES + plane * spare, spare, extra)
        place = plane % LEVELS
        folded = folded_in(folded if place else None, (low, high), place)
        if place == LEVELS - 1 or plane == PLANES - 1:
            fold = plane // LEVELS
            main, extra = pack_polar(*folded)
            beyond_ref[8 * fold : 8 * fold + 8, :] = main
            put_extra(beyond_ref, (), 8 * FOLDS + fold * polar_spare, polar_spare, extra)


def all_sums(spares, near_table, polar_table, mine, other):
    spare, polar_spare = spares
    return pl.pallas_call(
        functools.partial(all_kernel, spare, polar_spare),
        out_shape=(
            jax.ShapeDtypeStruct((SUMS, ROWS), f32),
            jax.ShapeDtypeStruct((padded((8 + spare) * PLANES), ROWS), f32),
            jax.ShapeDtypeStruct(((8 + polar_spare) * FOLDS, ROWS), f32),
        ),
        in_specs=[pl.BlockSpec(memory_space=VMEM)] * 4,
        out_specs=(pl.BlockSpec(memory_space=VMEM),) * 3,
        name="all_sums",
        compiler_params=PARAMS,
        cost_estimate=COST,
    )(near_table, polar_table, mine, other)


def organic_kernel(
    spare, polar_spare,
    shifts_ref, near_ref, polar_ref, own_ref, behind_ref, beyond_ref, mine_ref, other_ref, after_ref,
    out_ref,
):
    del after_ref
    shifts = jnp.broadcast_to(shifts_ref[...], (8, ROWS))
    masks = far_masks(shifts)
    is_polar = shifts >= CELLS
    near_lines, polar_lines = liner(near_ref, spare), liner(polar_ref, polar_spare)
    lanes = (table(near_ref, 3, 0), table(near_ref, 3, 1))
    spread = None
    for at, meta_ref in enumerate((mine_ref, other_ref)):
        meta = [
            [meta_ref[SUMS + 16 * n + 8 * h : SUMS + 16 * n + 8 * h + 8, :] for h in range(2)]
            for n in range(3)
        ]
        rest, frac, temp = meta
        advected = []
        for b in range(BINS):
            plane = BINS * at + b
            begin, fold, place = CELLS * plane, plane // LEVELS, plane % LEVELS
            own = (own_ref[begin : begin + 8, :], own_ref[begin + 8 : begin + 16, :])
            if place == 0:
                spread = polar_lines(
                    beyond_ref[8 * fold : 8 * fold + 8, :],
                    get_extra(beyond_ref, (), 8 * FOLDS + fold * polar_spare, polar_spare),
                )
            lines = near_lines(
                behind_ref[8 * plane : 8 * plane + 8, :],
                get_extra(behind_ref, (), 8 * PLANES + plane * spare, spare),
            )
            behind = [along_lanes(lines[h], lanes[h]) for h in range(2)]
            beyond = [along_lanes(spread[h], table(polar_ref, 3 + place, h)) for h in range(2)]
            far = far_of(own, behind, beyond, masks)
            near = near_of(far, jnp.where(is_polar, behind[0], own[0]))
            advected.append([rest[h] * near[h] + frac[h] * far[h] for h in range(2)])
        for half in range(2):
            base = (298.15 / temp[half]) * jnp.exp(
                HEAT_OF_BOILING * (1.0 / 298.15 - 1.0 / temp[half])
            )
            organic = SEED + sum(advected[b][half] for b in range(BINS))
            for _ in range(PITERS):
                ratio = base / organic
                organic = SEED + sum(
                    advected[b][half] / (1.0 + 10.0 ** (b - 3) * ratio) for b in range(BINS)
                )
            out_ref[at, 8 * half : 8 * half + 8, :] = rest[half]
            out_ref[at, 16 + 8 * half : 24 + 8 * half, :] = frac[half]
            out_ref[at, 32 + 8 * half : 40 + 8 * half, :] = base / organic


def organic_of(spares, shifts, near_table, polar_table, own, behind, beyond, mine, other, after):
    return pl.pallas_call(
        functools.partial(organic_kernel, *spares),
        out_shape=jax.ShapeDtypeStruct((2, 3 * CELLS, ROWS), f32),
        in_specs=[pl.BlockSpec(memory_space=VMEM)] * 8 + any_specs(1),
        out_specs=pl.BlockSpec(memory_space=VMEM),
        name="organic",
        compiler_params=PARAMS,
        cost_estimate=COST,
    )(shifts, near_table, polar_table, own, behind, beyond, mine, other, after)


def pack_kernel(
    spare, polar_spare, start, shifts_ref, near_ref, polar_ref, loads_ref, *rest
):
    ahead_ref, beyond_ref = rest[-2:]
    shifts = jnp.broadcast_to(shifts_ref[...], (8, ROWS))
    turn = turning(shifts)
    s = pl.program_id(0) + start

    pack_near, pack_polar = packer(near_ref, spare), packer(polar_ref, polar_spare)

    def body(b, totals):
        folded, sums = None, []
        for level in range(LEVELS):
            low, high = turned(
                loads_ref[s, b, level, 0:8, :], loads_ref[s, b, level, 8:16, :], turn
            )
            sums.append(totals[level] + (low + high))
            folded = folded_in(folded, (low, high), level)
            main, extra = pack_near(low, high)
            plane = b * LEVELS + level
            ahead_ref[0, pl.ds(pl.multiple_of(8 * plane, 8), 8), :] = main
            put_extra(ahead_ref, (0,), 8 * BINS * LEVELS + plane * spare, spare, extra)
        main, extra = pack_polar(*folded)
        beyond_ref[0, pl.ds(pl.multiple_of(8 * b, 8), 8), :] = main
        put_extra(beyond_ref, (0,), 8 * BINS + b * polar_spare, polar_spare, extra)
        return tuple(sums)

    totals = lax.fori_loop(0, BINS, body, (jnp.zeros((8, ROWS), f32),) * LEVELS, unroll=3)
    begin = (8 + spare) * BINS * LEVELS
    for level in range(LEVELS):
        ahead_ref[0, begin + level : begin + level + 1, :] = jnp.sum(
            totals[level], axis=0, keepdims=True
        )


def packed_rows(spare, polar_spare):
    return (
        padded((8 + spare) * BINS * LEVELS + LEVELS),
        (8 + polar_spare) * BINS,
    )


def whole_spec(shape):
    return pl.BlockSpec(shape, lambda i: (0,) * len(shape))


def pack(spares, start, count, shifts, near_table, polar_table, loads, after, before):
    rows, polar_rows = packed_rows(*spares)
    species = loads.shape[0]
    args = [shifts, near_table, polar_table, loads, *after]
    in_specs = [pl.BlockSpec(memory_space=VMEM)] * 4 + any_specs(len(after))
    aliases = {}
    if before is not None:
        aliases = {len(args): 1}
        args.append(before)
        in_specs.append(pl.BlockSpec(memory_space=pl.ANY))
    return pl.pallas_call(
        functools.partial(pack_kernel, *spares, start),
        grid=(count,),
        out_shape=(
            jax.ShapeDtypeStruct((count, rows, ROWS), f32),
            jax.ShapeDtypeStruct((species, polar_rows, ROWS), f32),
        ),
        in_specs=in_specs,
        out_specs=(
            pl.BlockSpec((1, rows, ROWS), lambda i: (i, 0, 0)),
            pl.BlockSpec((1, polar_rows, ROWS), lambda i: (i + start, 0, 0)),
        ),
        input_output_aliases=aliases,
        name=f"pack_{start}",
        compiler_params=PARAMS,
        cost_estimate=COST,
    )(*args)


def weights_kernel(me_ref, pair_ref, other_ref, diff_ref, near_w, far_w, solve, fracs):
    for half in range(2):
        at = slice(8 * half, 8 * half + 8)
        diffusive = [diff_ref[k, at, :] for k in range(LEVELS - 1)]
        nothing = jnp.zeros((8, ROWS), f32)
        lower = [nothing] + diffusive
        upper = diffusive + [nothing]
        previous = nothing
        for k in range(LEVELS):
            pivot = 1.0 + lower[k] + upper[k] - lower[k] * previous
            inverse = 1.0 / pivot
            previous = upper[k] * inverse
            solve[0, k, at, :] = inverse
            solve[1, k, at, :] = lower[k] * inverse
            solve[2, k, at, :] = previous
    for away in range(LEVELS):
        level_ref = (pair_ref, other_ref)[away & 1].at[away >> 1]
        level = jnp.bitwise_xor(me_ref[0], away)
        for half in range(2):
            at = slice(8 * half, 8 * half + 8)
            rest_of = level_ref[8 * half : 8 * half + 8, :]
            frac = level_ref[16 + 8 * half : 24 + 8 * half, :]
            ratio = level_ref[32 + 8 * half : 40 + 8 * half, :]
            fracs[level, at, :] = frac
            inverse = solve[0, level, at, :]
            near_top, far_top = rest_of * inverse, frac * inverse
            for b in range(BINS):
                weight = 1.0 / (1.0 + 10.0 ** (b - 3) * ratio)
                near_w[b, level, at, :] = near_top * weight
                far_w[b, level, at, :] = far_top * weight


def weights_of(me, pair, other, diffusive):
    block = (LEVELS, CELLS, ROWS)
    return pl.pallas_call(
        weights_kernel,
        out_shape=tuple(
            jax.ShapeDtypeStruct(shape, f32)
            for shape in ((BINS,) + block, (BINS,) + block, (3,) + block, block)
        ),
        in_specs=[pl.BlockSpec(memory_space=pltpu.SMEM)] + [pl.BlockSpec(memory_space=VMEM)] * 3,
        out_specs=(pl.BlockSpec(memory_space=VMEM),) * 4,
        name="weights",
        compiler_params=PARAMS,
        cost_estimate=COST,
    )(me, pair, other, diffusive)


def final_kernel(
    spare, polar_spare, start,
    shifts_ref, near_ref, polar_ref, near_w, far_w, solve, fracs, loads_ref, behind_ref, beyond_ref,
    *rest,
):
    particle_ref, flux_ref = rest[-2:]
    shifts = jnp.broadcast_to(shifts_ref[...], (8, ROWS))
    halves = (slice(0, 8), slice(8, 16))
    turn = turning(shifts)
    masks = far_masks(shifts)
    is_polar = shifts >= CELLS
    i = pl.program_id(0)
    s = i + start

    near_lines, polar_lines = liner(near_ref, spare), liner(polar_ref, polar_spare)
    lanes = (table(near_ref, 3, 0), table(near_ref, 3, 1))

    def body(b, carry):
        spread = polar_lines(
            beyond_ref[s, pl.ds(pl.multiple_of(8 * b, 8), 8), :],
            get_extra(beyond_ref, (s,), 8 * BINS + b * polar_spare, polar_spare),
        )
        forward = [None] * LEVELS
        previous = None
        sums = []
        for k in range(LEVELS):
            low, high = loads_ref[s, b, k, 0:8, :], loads_ref[s, b, k, 8:16, :]
            own = turned(low, high, turn)
            plane = b * LEVELS + k
            lines = near_lines(
                behind_ref[i, pl.ds(pl.multiple_of(8 * plane, 8), 8), :],
                get_extra(behind_ref, (i,), 8 * BINS * LEVELS + plane * spare, spare),
            )
            behind = [along_lanes(lines[h], lanes[h]) for h in range(2)]
            beyond = [along_lanes(spread[h], table(polar_ref, 3 + k, h)) for h in range(2)]
            far = far_of(own, behind, beyond, masks)
            first = jnp.where(is_polar, behind[0], own[0])
            near = near_of(far, first)
            terms = (far[0], far[1], first, low, high)
            sums.append(tuple(a + t for a, t in zip(carry[k], terms)))
            step = []
            for half, at in enumerate(halves):
                value = near_w[b, k, at, :] * near[half] + far_w[b, k, at, :] * far[half]
                if k:
                    value = value + solve[1, k, at, :] * previous[half]
                step.append(value)
            forward[k] = previous = step
        following = forward[LEVELS - 1]
        for half, at in enumerate(halves):
            particle_ref[0, b, LEVELS - 1, at, :] = following[half]
        for k in range(LEVELS - 2, -1, -1):
            following = [
                forward[k][half] + solve[2, k, at, :] * following[half]
                for half, at in enumerate(halves)
            ]
            for half, at in enumerate(halves):
                particle_ref[0, b, k, at, :] = following[half]
        return tuple(sums)

    zero = jnp.zeros((8, ROWS), f32)
    sums = lax.fori_loop(0, BINS, body, ((zero,) * 5,) * LEVELS, unroll=3)
    cell = vreg_iota(0)
    within = shifts & (CELLS - 1)
    for k in range(LEVELS):
        far0, far1, first, low, high = sums[k]
        near0, near1 = near_of((far0, far1), first)
        counted = jnp.where((cell >= 1) & (cell <= within), far0, 0.0) + jnp.where(
            cell + 8 <= within, far1, 0.0
        )
        window = jnp.sum(counted, axis=0, keepdims=True)
        begin = (8 + spare) * BINS * LEVELS + k
        window = window + jnp.where(
            shifts_ref[...] >= CELLS, behind_ref[i, begin : begin + 1, :], 0.0
        )
        base = jnp.broadcast_to(window, (8, ROWS))
        for half, (gained, lost, far) in enumerate(((low, near0, far0), (high, near1, far1))):
            change = gained - lost
            running = change
            for step in (1, 2, 4):
                running = running + jnp.where(cell >= step, pltpu.roll(running, step, 0), 0.0)
            at = halves[half]
            flux_ref[0, k, at, :] = base + (running - change) + fracs[k, at, :] * far
            if half == 0:
                base = base + jnp.broadcast_to(running[7:8, :], (8, ROWS))


def final(
    spares, start, count, shifts, near_table, polar_table, weights, loads, behind, beyond, before
):
    species = loads.shape[0]
    outs = (
        jax.ShapeDtypeStruct((species, BINS, LEVELS, CELLS, ROWS), f32),
        jax.ShapeDtypeStruct((species, LEVELS, CELLS, ROWS), f32),
    )
    args = [shifts, near_table, polar_table, *weights, loads, behind, beyond]
    in_specs = [pl.BlockSpec(memory_space=VMEM)] * len(args)
    aliases = {}
    if before is not None:
        aliases = {len(args): 0, len(args) + 1: 1}
        args += list(before)
        in_specs += [pl.BlockSpec(memory_space=pl.ANY)] * 2
    return pl.pallas_call(
        functools.partial(final_kernel, *spares, start),
        grid=(count,),
        out_shape=outs,
        in_specs=in_specs,
        out_specs=(
            pl.BlockSpec((1, BINS, LEVELS, CELLS, ROWS), lambda i: (i + start, 0, 0, 0, 0)),
            pl.BlockSpec((1, LEVELS, CELLS, ROWS), lambda i: (i + start, 0, 0, 0)),
        ),
        input_output_aliases=aliases,
        name=f"final_{start}",
        compiler_params=PARAMS,
        cost_estimate=COST,
    )(*args)


def along_meridian(block):
    size = lax.axis_size("lon")
    return lax.ppermute(block, "lon", [(i, (i + 2) % size) for i in range(1, size, 2)])


def crossed(block):
    return lax.ppermute(block, "lon", [(i, i ^ 1) for i in range(lax.axis_size("lon"))])


def pipeline(spares, me, shifts, near_table, polar_table, loads, frac, temp, diffusive):
    tables = (shifts, near_table, polar_table)
    odd = lax.axis_index("lon") % 2 == 1
    starts = [sum(CHUNKS[:i]) for i in range(len(CHUNKS))]
    last = len(CHUNKS) - 1
    east = from_behind(frac[:, :1, :], "lon", -1)
    keep, send = species_sums(me, shifts, loads, near_table)
    got = swapped(send, 1)
    mine = chip_sums(keep, got, frac, east, temp)
    other = swapped(mine, 2)
    own, ahead_sums, beyond_sums = all_sums(spares, near_table, polar_table, mine, other)
    after, beyond, aheads = [keep], None, [None] * len(CHUNKS)
    for at in (0, last, 2, 1):
        aheads[at], beyond = pack(
            spares, starts[at], CHUNKS[at], *tables, loads, after, beyond
        )
        after = [aheads[at], own] if at == 2 else [aheads[at]]
    relayed = along_meridian(aheads[last])
    aheads[0], _ = lax.optimization_barrier((aheads[0], mine))
    behind = [from_behind(aheads[0], "lon", 1), from_behind(aheads[1], "lon", 1)]
    sums_behind = from_behind(ahead_sums, "lon", 1)
    sums_beyond = from_behind(beyond_sums, "lon", 2)
    beyond = from_behind(beyond, "lon", 2)
    aheads[2], behind[0] = lax.optimization_barrier((aheads[2], behind[0]))
    behind.append(from_behind(aheads[2], "lon", 1))
    mixed, sums_behind, sums_beyond = lax.optimization_barrier(
        (jnp.where(odd, relayed, aheads[last]), sums_behind, sums_beyond)
    )
    behind.append(crossed(mixed))
    level = organic_of(spares, *tables, own, sums_behind, sums_beyond, mine, other, behind[0])
    weights = weights_of(me, level, swapped(level, 1), diffusive)
    outs = None
    for start, count, block in zip(starts, CHUNKS, behind):
        outs = final(spares, start, count, *tables, weights, loads, block, beyond, outs)
    return tuple(outs)


def per_device(loads, frac, temp, diffusive, whole_shifts):
    me = lax.axis_index("spc").astype(i32).reshape(1)
    shifts = whole_shifts.reshape(1, ROWS)
    near_table, polar_table, which = make_tables(shifts)
    branches = [functools.partial(pipeline, spares) for spares in SPARES]
    return lax.switch(
        which[0], branches, me, shifts, near_table, polar_table, loads, frac, temp, diffusive
    )


def solution(mesh):
    placed = (
        P("spc", None, None, "lon", None),
        P("spc", "lon", None),
        P("spc", "lon", None),
        P(None, "lon", None),
        P(),
    )
    return jax.shard_map(
        per_device,
        mesh=mesh,
        in_specs=placed,
        out_specs=(P("spc", None, None, "lon", None), P("spc", None, "lon", None)),
        check_vma=False,
    )
```

```python
import functools

import jax
import jax.numpy as jnp
from jax import lax
from jax.experimental import pallas as pl
from jax.experimental.pallas import tpu as pltpu
from jax.sharding import PartitionSpec as P

BINS = 9
LEVELS = 4
PITERS = 2
CELLS = 16
ROWS = 128
POLAR = 32
SEED = 1.0
HEAT_OF_BOILING = 5000.0
CHUNKS = (2, 3, 2, 3)
SPARES = ((1, 0), (2, 0), (8, 8))

VMEM = pltpu.VMEM
COST = pl.CostEstimate(flops=1, bytes_accessed=1, transcendentals=0)
PARAMS = pltpu.CompilerParams(vmem_limit_bytes=16 * 2**20)
f32, i32 = jnp.float32, jnp.int32


def from_behind(block, axis, distance):
    devices = range(lax.axis_size(axis))
    route = [((i - distance) % len(devices), i) for i in devices]
    return lax.ppermute(block, axis, route)


def swapped(block, mask):
    route = [(i, i ^ mask) for i in range(lax.axis_size("spc"))]
    return lax.ppermute(block, "spc", route)


def any_specs(count):
    return [pl.BlockSpec(memory_space=pl.ANY)] * count


def along_lanes(values, index):
    return jnp.take_along_axis(values, index, axis=1, mode="promise_in_bounds")


def along_cells(values, index):
    return jnp.take_along_axis(values, index, axis=0, mode="promise_in_bounds")


def vreg_iota(dim):
    return lax.broadcasted_iota(i32, (8, ROWS), dim)


def padded(rows):
    return -(-rows // 8) * 8


def packing(needed):
    ones = jnp.where(needed, 1.0, 0.0).astype(jnp.bfloat16)
    row = lax.broadcasted_iota(i32, (ROWS, ROWS), 0)
    lane = lax.broadcasted_iota(i32, (ROWS, ROWS), 1)
    upto = jnp.where(row <= lane, 1.0, 0.0).astype(jnp.bfloat16)
    ranked = jnp.dot(ones, upto, preferred_element_type=f32).astype(i32)
    count = jnp.sum(jnp.where(needed, 1, 0), axis=1, keepdims=True)
    offsets, running = [], jnp.zeros((1, 1), i32)
    for cell in range(CELLS):
        offsets.append(running)
        running = running + count[cell : cell + 1]
    ends = offsets[1:] + [running]
    offset = jnp.concatenate(offsets, axis=0)
    lanes = lax.broadcasted_iota(i32, (CELLS, ROWS), 1)
    heights = lax.broadcasted_iota(i32, (CELLS, ROWS), 0)
    flat = offset + ranked - 1
    unpack_lane = flat & 127
    unpack_row = (offset >> 7) + jnp.where(lanes < (offset & 127), 1, 0)
    place = heights * ROWS + lanes
    pack_row = jnp.zeros((CELLS, ROWS), i32)
    for cell in range(CELLS):
        pack_row = pack_row + jnp.where(place >= ends[cell], 1, 0)
    pack_row = jnp.minimum(pack_row, CELLS - 1)
    wanted = (lanes - offset) & 127
    halves = []
    for half in range(2):
        at = slice(8 * half, 8 * half + 8)
        position = jnp.zeros((8, ROWS), i32)
        for step in (64, 32, 16, 8, 4, 2, 1):
            probe = along_lanes(ranked[at], position + (step - 1))
            position = jnp.where(probe <= wanted[at], position + step, position)
        halves.append(position)
    return (jnp.concatenate(halves, axis=0), pack_row, unpack_row, unpack_lane), running


def tables_kernel(shifts_ref, near_ref, polar_ref, which_ref):
    shifts = jnp.broadcast_to(shifts_ref[...], (CELLS, ROWS))
    cell = lax.broadcasted_iota(i32, (CELLS, ROWS), 0)
    needed = jnp.where(
        shifts < CELLS, jnp.where(cell <= shifts, 1, 0),
        jnp.where((cell == 0) | (cell > shifts - CELLS), 1, 0),
    ) > 0
    made, near_cells = packing(needed)
    for at, table in enumerate(made):
        near_ref[CELLS * at : CELLS * at + CELLS, :] = table
    within = vreg_iota(1) & (POLAR - 1)
    folded = along_lanes(shifts[:8], within)
    folded = jnp.concatenate([folded, folded], axis=0)
    needed = cell <= folded - CELLS
    (pack_lane, pack_row, unpack_row, unpack_lane), polar_cells = packing(needed)
    near_cells, polar_cells = jnp.sum(near_cells), jnp.sum(polar_cells)
    which_ref[0] = sum(
        jnp.where((near_cells > ROWS * (8 + a)) | (polar_cells > ROWS * (8 + c)), 1, 0)
        for a, c in SPARES[:-1]
    )
    polar_ref[0:16, :] = pack_lane
    polar_ref[16:32, :] = pack_row
    polar_ref[32:48, :] = unpack_row
    for level in range(LEVELS):
        for half in range(2):
            start = 48 + CELLS * level + 8 * half
            polar_ref[start : start + 8, :] = along_lanes(
                unpack_lane[8 * half : 8 * half + 8], within + POLAR * level
            )


def make_tables(shifts):
    return pl.pallas_call(
        tables_kernel,
        out_shape=(
            jax.ShapeDtypeStruct((4 * CELLS, ROWS), i32),
            jax.ShapeDtypeStruct((3 * CELLS + LEVELS * CELLS, ROWS), i32),
            jax.ShapeDtypeStruct((1,), i32),
        ),
        out_specs=(
            pl.BlockSpec(memory_space=VMEM),
            pl.BlockSpec(memory_space=VMEM),
            pl.BlockSpec(memory_space=pltpu.SMEM),
        ),
        name="tables",
        compiler_params=PARAMS,
    )(shifts)


def turning(shifts):
    back = vreg_iota(0) - shifts - 1
    return back & 7, (back & 15) >= 8


def turned(low, high, turn):
    index, swap = turn
    low, high = along_cells(low, index), along_cells(high, index)
    return jnp.where(swap, high, low), jnp.where(swap, low, high)


def far_masks(shifts):
    cell = vreg_iota(0)
    masks = []
    for half in range(2):
        at = cell + 8 * half
        polar = at <= shifts - CELLS
        behind = at <= shifts
        masks.append((behind, polar))
    return masks


def near_of(far, first):
    last = vreg_iota(0) == 7
    rolled = [pltpu.roll(half, 7, 0) for half in (far[0], far[1], first)]
    return (
        jnp.where(last, rolled[1], rolled[0]),
        jnp.where(last, rolled[2], rolled[1]),
    )


def table(ref, which, half):
    begin = CELLS * which + 8 * half
    return ref[begin : begin + 8, :]


def packer(table_ref, spare):
    lanes = (table(table_ref, 0, 0), table(table_ref, 0, 1))
    rows = table(table_ref, 1, 0)
    later = jnp.maximum(table(table_ref, 1, 1) - 8, 0)
    early, rows = rows < 8, rows & 7

    def pack_plane(low, high):
        low, high = along_lanes(low, lanes[0]), along_lanes(high, lanes[1])
        main = jnp.where(early, along_cells(low, rows), along_cells(high, rows))
        return main, along_cells(high, later) if spare else None

    return pack_plane


def folded_in(before, plane, place):
    if before is None:
        return list(plane)
    here = vreg_iota(1) >= POLAR * place
    return [
        jnp.where(here, pltpu.roll(half, POLAR * place, 1), old)
        for half, old in zip(plane, before)
    ]


def put_extra(ref, lead, begin, spare, extra):
    if spare == 8:
        ref[(*lead, pl.ds(pl.multiple_of(begin, 8), 8), slice(None))] = extra
    else:
        for row in range(spare):
            ref[(*lead, pl.ds(begin + row, 1), slice(None))] = extra[row : row + 1]


def get_extra(ref, lead, begin, spare):
    if spare == 8:
        return [ref[(*lead, pl.ds(pl.multiple_of(begin, 8), 8), slice(None))]]
    return [
        jnp.broadcast_to(ref[(*lead, pl.ds(begin + row, 1), slice(None))], (8, ROWS))
        for row in range(spare)
    ]


def liner(table_ref, spare):
    row0, row1 = table(table_ref, 2, 0) & 7, table(table_ref, 2, 1)
    low_row, late_row = row1 & 7, row1 >= 8

    def lines(main, extra):
        low, high = along_cells(main, row0), along_cells(main, low_row)
        if spare == 8:
            high = jnp.where(late_row, along_cells(extra[0], low_row), high)
        else:
            for row, late in enumerate(extra):
                high = jnp.where(row1 == 8 + row, late, high)
        return [low, high]

    return lines


def far_of(own, behind, beyond, masks):
    return [
        jnp.where(masks[h][1], beyond[h], jnp.where(masks[h][0], behind[h], own[h]))
        for h in range(2)
    ]


def species_kernel(me_ref, shifts_ref, loads_ref, after_ref, keep_ref, send_ref):
    del after_ref
    shifts = jnp.broadcast_to(shifts_ref[...], (8, ROWS))
    turn = turning(shifts)
    species = loads_ref.shape[0]

    def body(b, carry):
        for away, (part, at) in enumerate(((keep_ref, 0), (send_ref, 0), (keep_ref, 1), (send_ref, 1))):
            level = jnp.bitwise_xor(me_ref[0], away)
            low = sum(loads_ref[s, b, level, 0:8, :] for s in range(1, species))
            high = sum(loads_ref[s, b, level, 8:16, :] for s in range(1, species))
            low = low + loads_ref[0, b, level, 0:8, :]
            high = high + loads_ref[0, b, level, 8:16, :]
            low, high = turned(low, high, turn)
            part[at, b, 0:8, :] = low
            part[at, b, 8:16, :] = high
        return carry

    lax.fori_loop(0, BINS, body, 0)


def species_sums(me, shifts, loads, after):
    return pl.pallas_call(
        species_kernel,
        out_shape=(jax.ShapeDtypeStruct((2, BINS, CELLS, ROWS), f32),) * 2,
        in_specs=[
            pl.BlockSpec(memory_space=pltpu.SMEM),
            pl.BlockSpec(memory_space=VMEM),
            pl.BlockSpec(memory_space=VMEM),
        ]
        + any_specs(1),
        out_specs=(pl.BlockSpec(memory_space=VMEM),) * 2,
        name="species_sums",
        compiler_params=PARAMS,
        cost_estimate=COST,
    )(me, shifts, loads, after)


PLANES = 2 * BINS
SUMS = PLANES * CELLS
FOLDS = -(-PLANES // LEVELS)


def chip_kernel(keep_ref, got_ref, frac_ref, east_ref, temp_ref, out_ref):
    for at in range(2):
        for b in range(BINS):
            begin = CELLS * (BINS * at + b)
            out_ref[begin : begin + CELLS, :] = keep_ref[at, b] + got_ref[at, b]
    frac = (frac_ref[0, 0:8, :], frac_ref[0, 8:16, :])
    east = near_of(frac, jnp.broadcast_to(east_ref[0], (8, ROWS)))
    for half in range(2):
        begin = SUMS + 8 * half
        out_ref[begin : begin + 8, :] = 1.0 - east[half]
        out_ref[begin + 16 : begin + 24, :] = frac[half]
        out_ref[begin + 32 : begin + 40, :] = temp_ref[0, 8 * half : 8 * half + 8, :]


def chip_sums(keep, got, frac, east, temp):
    return pl.pallas_call(
        chip_kernel,
        out_shape=jax.ShapeDtypeStruct((SUMS + 3 * CELLS, ROWS), f32),
        in_specs=[pl.BlockSpec(memory_space=VMEM)] * 5,
        out_specs=pl.BlockSpec(memory_space=VMEM),
        name="chip_sums",
        compiler_params=PARAMS,
        cost_estimate=COST,
    )(keep, got, frac, east, temp)


def all_kernel(spare, polar_spare, near_ref, polar_ref, mine_ref, other_ref, own_ref, ahead_ref, beyond_ref):
    pack_near, pack_polar = packer(near_ref, spare), packer(polar_ref, polar_spare)
    folded = None
    for plane in range(PLANES):
        begin = CELLS * plane
        across = CELLS * ((plane + BINS) % PLANES)
        low = mine_ref[begin : begin + 8, :] + other_ref[across : across + 8, :]
        high = mine_ref[begin + 8 : begin + 16, :] + other_ref[across + 8 : across + 16, :]
        own_ref[begin : begin + 8, :] = low
        own_ref[begin + 8 : begin + 16, :] = high
        main, extra = pack_near(low, high)
        ahead_ref[8 * plane : 8 * plane + 8, :] = main
        put_extra(ahead_ref, (), 8 * PLANES + plane * spare, spare, extra)
        place = plane % LEVELS
        folded = folded_in(folded if place else None, (low, high), place)
        if place == LEVELS - 1 or plane == PLANES - 1:
            fold = plane // LEVELS
            main, extra = pack_polar(*folded)
            beyond_ref[8 * fold : 8 * fold + 8, :] = main
            put_extra(beyond_ref, (), 8 * FOLDS + fold * polar_spare, polar_spare, extra)


def all_sums(spares, near_table, polar_table, mine, other):
    spare, polar_spare = spares
    return pl.pallas_call(
        functools.partial(all_kernel, spare, polar_spare),
        out_shape=(
            jax.ShapeDtypeStruct((SUMS, ROWS), f32),
            jax.ShapeDtypeStruct((padded((8 + spare) * PLANES), ROWS), f32),
            jax.ShapeDtypeStruct(((8 + polar_spare) * FOLDS, ROWS), f32),
        ),
        in_specs=[pl.BlockSpec(memory_space=VMEM)] * 4,
        out_specs=(pl.BlockSpec(memory_space=VMEM),) * 3,
        name="all_sums",
        compiler_params=PARAMS,
        cost_estimate=COST,
    )(near_table, polar_table, mine, other)


def organic_kernel(
    spare, polar_spare,
    shifts_ref, near_ref, polar_ref, own_ref, behind_ref, beyond_ref, mine_ref, other_ref, after_ref,
    out_ref,
):
    del after_ref
    shifts = jnp.broadcast_to(shifts_ref[...], (8, ROWS))
    masks = far_masks(shifts)
    is_polar = shifts >= CELLS
    near_lines, polar_lines = liner(near_ref, spare), liner(polar_ref, polar_spare)
    lanes = (table(near_ref, 3, 0), table(near_ref, 3, 1))
    spread = None
    for at, meta_ref in enumerate((mine_ref, other_ref)):
        meta = [
            [meta_ref[SUMS + 16 * n + 8 * h : SUMS + 16 * n + 8 * h + 8, :] for h in range(2)]
            for n in range(3)
        ]
        rest, frac, temp = meta
        advected = []
        for b in range(BINS):
            plane = BINS * at + b
            begin, fold, place = CELLS * plane, plane // LEVELS, plane % LEVELS
            own = (own_ref[begin : begin + 8, :], own_ref[begin + 8 : begin + 16, :])
            if place == 0:
                spread = polar_lines(
                    beyond_ref[8 * fold : 8 * fold + 8, :],
                    get_extra(beyond_ref, (), 8 * FOLDS + fold * polar_spare, polar_spare),
                )
            lines = near_lines(
                behind_ref[8 * plane : 8 * plane + 8, :],
                get_extra(behind_ref, (), 8 * PLANES + plane * spare, spare),
            )
            behind = [along_lanes(lines[h], lanes[h]) for h in range(2)]
            beyond = [along_lanes(spread[h], table(polar_ref, 3 + place, h)) for h in range(2)]
            far = far_of(own, behind, beyond, masks)
            near = near_of(far, jnp.where(is_polar, behind[0], own[0]))
            advected.append([rest[h] * near[h] + frac[h] * far[h] for h in range(2)])
        for half in range(2):
            base = (298.15 / temp[half]) * jnp.exp(
                HEAT_OF_BOILING * (1.0 / 298.15 - 1.0 / temp[half])
            )
            organic = SEED + sum(advected[b][half] for b in range(BINS))
            for _ in range(PITERS):
                ratio = base / organic
                organic = SEED + sum(
                    advected[b][half] / (1.0 + 10.0 ** (b - 3) * ratio) for b in range(BINS)
                )
            out_ref[at, 8 * half : 8 * half + 8, :] = rest[half]
            out_ref[at, 16 + 8 * half : 24 + 8 * half, :] = frac[half]
            out_ref[at, 32 + 8 * half : 40 + 8 * half, :] = base / organic


def organic_of(spares, shifts, near_table, polar_table, own, behind, beyond, mine, other, after):
    return pl.pallas_call(
        functools.partial(organic_kernel, *spares),
        out_shape=jax.ShapeDtypeStruct((2, 3 * CELLS, ROWS), f32),
        in_specs=[pl.BlockSpec(memory_space=VMEM)] * 8 + any_specs(1),
        out_specs=pl.BlockSpec(memory_space=VMEM),
        name="organic",
        compiler_params=PARAMS,
        cost_estimate=COST,
    )(shifts, near_table, polar_table, own, behind, beyond, mine, other, after)


def pack_kernel(
    spare, polar_spare, start, shifts_ref, near_ref, polar_ref, loads_ref, *rest
):
    ahead_ref, beyond_ref = rest[-2:]
    shifts = jnp.broadcast_to(shifts_ref[...], (8, ROWS))
    turn = turning(shifts)
    s = pl.program_id(0) + start

    pack_near, pack_polar = packer(near_ref, spare), packer(polar_ref, polar_spare)

    def body(b, totals):
        folded, sums = None, []
        for level in range(LEVELS):
            low, high = turned(
                loads_ref[s, b, level, 0:8, :], loads_ref[s, b, level, 8:16, :], turn
            )
            sums.append(totals[level] + (low + high))
            folded = folded_in(folded, (low, high), level)
            main, extra = pack_near(low, high)
            plane = b * LEVELS + level
            ahead_ref[0, pl.ds(pl.multiple_of(8 * plane, 8), 8), :] = main
            put_extra(ahead_ref, (0,), 8 * BINS * LEVELS + plane * spare, spare, extra)
        main, extra = pack_polar(*folded)
        beyond_ref[0, pl.ds(pl.multiple_of(8 * b, 8), 8), :] = main
        put_extra(beyond_ref, (0,), 8 * BINS + b * polar_spare, polar_spare, extra)
        return tuple(sums)

    totals = lax.fori_loop(0, BINS, body, (jnp.zeros((8, ROWS), f32),) * LEVELS, unroll=3)
    begin = (8 + spare) * BINS * LEVELS
    for level in range(LEVELS):
        ahead_ref[0, begin + level : begin + level + 1, :] = jnp.sum(
            totals[level], axis=0, keepdims=True
        )


def packed_rows(spare, polar_spare):
    return (
        padded((8 + spare) * BINS * LEVELS + LEVELS),
        (8 + polar_spare) * BINS,
    )


def whole_spec(shape):
    return pl.BlockSpec(shape, lambda i: (0,) * len(shape))


def pack(spares, start, count, shifts, near_table, polar_table, loads, after, before):
    rows, polar_rows = packed_rows(*spares)
    species = loads.shape[0]
    args = [shifts, near_table, polar_table, loads, *after]
    in_specs = [pl.BlockSpec(memory_space=VMEM)] * 4 + any_specs(len(after))
    aliases = {}
    if before is not None:
        aliases = {len(args): 1}
        args.append(before)
        in_specs.append(pl.BlockSpec(memory_space=pl.ANY))
    return pl.pallas_call(
        functools.partial(pack_kernel, *spares, start),
        grid=(count,),
        out_shape=(
            jax.ShapeDtypeStruct((count, rows, ROWS), f32),
            jax.ShapeDtypeStruct((species, polar_rows, ROWS), f32),
        ),
        in_specs=in_specs,
        out_specs=(
            pl.BlockSpec((1, rows, ROWS), lambda i: (i, 0, 0)),
            pl.BlockSpec((1, polar_rows, ROWS), lambda i: (i + start, 0, 0)),
        ),
        input_output_aliases=aliases,
        name=f"pack_{start}",
        compiler_params=PARAMS,
        cost_estimate=COST,
    )(*args)


def weights_kernel(me_ref, pair_ref, other_ref, diff_ref, near_w, far_w, solve, fracs):
    for half in range(2):
        at = slice(8 * half, 8 * half + 8)
        diffusive = [diff_ref[k, at, :] for k in range(LEVELS - 1)]
        nothing = jnp.zeros((8, ROWS), f32)
        lower = [nothing] + diffusive
        upper = diffusive + [nothing]
        previous = nothing
        for k in range(LEVELS):
            pivot = 1.0 + lower[k] + upper[k] - lower[k] * previous
            inverse = 1.0 / pivot
            previous = upper[k] * inverse
            solve[0, k, at, :] = inverse
            solve[1, k, at, :] = lower[k] * inverse
            solve[2, k, at, :] = previous
    for away in range(LEVELS):
        level_ref = (pair_ref, other_ref)[away & 1].at[away >> 1]
        level = jnp.bitwise_xor(me_ref[0], away)
        for half in range(2):
            at = slice(8 * half, 8 * half + 8)
            rest_of = level_ref[8 * half : 8 * half + 8, :]
            frac = level_ref[16 + 8 * half : 24 + 8 * half, :]
            ratio = level_ref[32 + 8 * half : 40 + 8 * half, :]
            fracs[level, at, :] = frac
            inverse = solve[0, level, at, :]
            near_top, far_top = rest_of * inverse, frac * inverse
            for b in range(BINS):
                weight = 1.0 / (1.0 + 10.0 ** (b - 3) * ratio)
                near_w[b, level, at, :] = near_top * weight
                far_w[b, level, at, :] = far_top * weight


def weights_of(me, pair, other, diffusive):
    block = (LEVELS, CELLS, ROWS)
    return pl.pallas_call(
        weights_kernel,
        out_shape=tuple(
            jax.ShapeDtypeStruct(shape, f32)
            for shape in ((BINS,) + block, (BINS,) + block, (3,) + block, block)
        ),
        in_specs=[pl.BlockSpec(memory_space=pltpu.SMEM)] + [pl.BlockSpec(memory_space=VMEM)] * 3,
        out_specs=(pl.BlockSpec(memory_space=VMEM),) * 4,
        name="weights",
        compiler_params=PARAMS,
        cost_estimate=COST,
    )(me, pair, other, diffusive)


def final_kernel(
    spare, polar_spare, start,
    shifts_ref, near_ref, polar_ref, near_w, far_w, solve, fracs, loads_ref, behind_ref, beyond_ref,
    *rest,
):
    particle_ref, flux_ref = rest[-2:]
    shifts = jnp.broadcast_to(shifts_ref[...], (8, ROWS))
    halves = (slice(0, 8), slice(8, 16))
    turn = turning(shifts)
    masks = far_masks(shifts)
    is_polar = shifts >= CELLS
    i = pl.program_id(0)
    s = i + start

    near_lines, polar_lines = liner(near_ref, spare), liner(polar_ref, polar_spare)
    lanes = (table(near_ref, 3, 0), table(near_ref, 3, 1))

    def body(b, carry):
        spread = polar_lines(
            beyond_ref[s, pl.ds(pl.multiple_of(8 * b, 8), 8), :],
            get_extra(beyond_ref, (s,), 8 * BINS + b * polar_spare, polar_spare),
        )
        forward = [None] * LEVELS
        previous = None
        sums = []
        for k in range(LEVELS):
            low, high = loads_ref[s, b, k, 0:8, :], loads_ref[s, b, k, 8:16, :]
            own = turned(low, high, turn)
            plane = b * LEVELS + k
            lines = near_lines(
                behind_ref[i, pl.ds(pl.multiple_of(8 * plane, 8), 8), :],
                get_extra(behind_ref, (i,), 8 * BINS * LEVELS + plane * spare, spare),
            )
            behind = [along_lanes(lines[h], lanes[h]) for h in range(2)]
            beyond = [along_lanes(spread[h], table(polar_ref, 3 + k, h)) for h in range(2)]
            far = far_of(own, behind, beyond, masks)
            first = jnp.where(is_polar, behind[0], own[0])
            near = near_of(far, first)
            terms = (far[0], far[1], first, low, high)
            sums.append(tuple(a + t for a, t in zip(carry[k], terms)))
            step = []
            for half, at in enumerate(halves):
                value = near_w[b, k, at, :] * near[half] + far_w[b, k, at, :] * far[half]
                if k:
                    value = value + solve[1, k, at, :] * previous[half]
                step.append(value)
            forward[k] = previous = step
        following = forward[LEVELS - 1]
        for half, at in enumerate(halves):
            particle_ref[0, b, LEVELS - 1, at, :] = following[half]
        for k in range(LEVELS - 2, -1, -1):
            following = [
                forward[k][half] + solve[2, k, at, :] * following[half]
                for half, at in enumerate(halves)
            ]
            for half, at in enumerate(halves):
                particle_ref[0, b, k, at, :] = following[half]
        return tuple(sums)

    zero = jnp.zeros((8, ROWS), f32)
    sums = lax.fori_loop(0, BINS, body, ((zero,) * 5,) * LEVELS, unroll=3)
    cell = vreg_iota(0)
    within = shifts & (CELLS - 1)
    for k in range(LEVELS):
        far0, far1, first, low, high = sums[k]
        near0, near1 = near_of((far0, far1), first)
        counted = jnp.where((cell >= 1) & (cell <= within), far0, 0.0) + jnp.where(
            cell + 8 <= within, far1, 0.0
        )
        window = jnp.sum(counted, axis=0, keepdims=True)
        begin = (8 + spare) * BINS * LEVELS + k
        window = window + jnp.where(
            shifts_ref[...] >= CELLS, behind_ref[i, begin : begin + 1, :], 0.0
        )
        base = jnp.broadcast_to(window, (8, ROWS))
        for half, (gained, lost, far) in enumerate(((low, near0, far0), (high, near1, far1))):
            change = gained - lost
            running = change
            for step in (1, 2, 4):
                running = running + jnp.where(cell >= step, pltpu.roll(running, step, 0), 0.0)
            at = halves[half]
            flux_ref[0, k, at, :] = base + (running - change) + fracs[k, at, :] * far
            if half == 0:
                base = base + jnp.broadcast_to(running[7:8, :], (8, ROWS))


def final(
    spares, start, count, shifts, near_table, polar_table, weights, loads, behind, beyond, before
):
    species = loads.shape[0]
    outs = (
        jax.ShapeDtypeStruct((species, BINS, LEVELS, CELLS, ROWS), f32),
        jax.ShapeDtypeStruct((species, LEVELS, CELLS, ROWS), f32),
    )
    args = [shifts, near_table, polar_table, *weights, loads, behind, beyond]
    in_specs = [pl.BlockSpec(memory_space=VMEM)] * len(args)
    aliases = {}
    if before is not None:
        aliases = {len(args): 0, len(args) + 1: 1}
        args += list(before)
        in_specs += [pl.BlockSpec(memory_space=pl.ANY)] * 2
    return pl.pallas_call(
        functools.partial(final_kernel, *spares, start),
        grid=(count,),
        out_shape=outs,
        in_specs=in_specs,
        out_specs=(
            pl.BlockSpec((1, BINS, LEVELS, CELLS, ROWS), lambda i: (i + start, 0, 0, 0, 0)),
            pl.BlockSpec((1, LEVELS, CELLS, ROWS), lambda i: (i + start, 0, 0, 0)),
        ),
        input_output_aliases=aliases,
        name=f"final_{start}",
        compiler_params=PARAMS,
        cost_estimate=COST,
    )(*args)


def along_meridian(block):
    size = lax.axis_size("lon")
    return lax.ppermute(block, "lon", [(i, (i + 2) % size) for i in range(1, size, 2)])


def crossed(block):
    return lax.ppermute(block, "lon", [(i, i ^ 1) for i in range(lax.axis_size("lon"))])


def pipeline(spares, me, shifts, near_table, polar_table, loads, frac, temp, diffusive):
    tables = (shifts, near_table, polar_table)
    odd = lax.axis_index("lon") % 2 == 1
    starts = [sum(CHUNKS[:i]) for i in range(len(CHUNKS))]
    last = len(CHUNKS) - 1
    east = from_behind(frac[:, :1, :], "lon", -1)
    keep, send = species_sums(me, shifts, loads, near_table)
    got = swapped(send, 1)
    mine = chip_sums(keep, got, frac, east, temp)
    other = swapped(mine, 2)
    own, ahead_sums, beyond_sums = all_sums(spares, near_table, polar_table, mine, other)
    after, beyond, aheads = [keep], None, [None] * len(CHUNKS)
    for at in (0, last, 2, 1):
        aheads[at], beyond = pack(
            spares, starts[at], CHUNKS[at], *tables, loads, after, beyond
        )
        after = [aheads[at]] + {0: [mine], 2: [own]}.get(at, [])
    relayed = along_meridian(aheads[last])
    aheads[0], _ = lax.optimization_barrier((aheads[0], mine))
    behind = [from_behind(aheads[0], "lon", 1), from_behind(aheads[1], "lon", 1)]
    sums_behind = from_behind(ahead_sums, "lon", 1)
    sums_beyond = from_behind(beyond_sums, "lon", 2)
    beyond = from_behind(beyond, "lon", 2)
    aheads[2], aheads[1], behind[0] = lax.optimization_barrier(
        (aheads[2], aheads[1], behind[0])
    )
    behind.append(from_behind(aheads[2], "lon", 1))
    mixed, _, sums_behind, sums_beyond = lax.optimization_barrier(
        (jnp.where(odd, relayed, aheads[last]), aheads[1], sums_behind, sums_beyond)
    )
    behind.append(crossed(mixed))
    level = organic_of(spares, *tables, own, sums_behind, sums_beyond, mine, other, behind[0])
    weights = weights_of(me, level, swapped(level, 1), diffusive)
    outs = None
    for at in (0, 1, last, 2):
        outs = final(
            spares, starts[at], CHUNKS[at], *tables, weights, loads, behind[at], beyond, outs
        )
    return tuple(outs)


def per_device(loads, frac, temp, diffusive, whole_shifts):
    me = lax.axis_index("spc").astype(i32).reshape(1)
    shifts = whole_shifts.reshape(1, ROWS)
    near_table, polar_table, which = make_tables(shifts)
    branches = [functools.partial(pipeline, spares) for spares in SPARES]
    return lax.switch(
        which[0], branches, me, shifts, near_table, polar_table, loads, frac, temp, diffusive
    )


def solution(mesh):
    placed = (
        P("spc", None, None, "lon", None),
        P("spc", "lon", None),
        P("spc", "lon", None),
        P(None, "lon", None),
        P(),
    )
    return jax.shard_map(
        per_device,
        mesh=mesh,
        in_specs=placed,
        out_specs=(P("spc", None, None, "lon", None), P("spc", None, "lon", None)),
        check_vma=False,
    )
```

```python
import functools

import jax
import jax.numpy as jnp
from jax import lax
from jax.experimental import pallas as pl
from jax.experimental.pallas import tpu as pltpu
from jax.sharding import PartitionSpec as P

BINS = 9
LEVELS = 4
PITERS = 2
CELLS = 16
ROWS = 128
POLAR = 32
SEED = 1.0
HEAT_OF_BOILING = 5000.0
CHUNKS = (2, 3, 3, 2)
SPARES = ((1, 0), (2, 0), (8, 8))

VMEM = pltpu.VMEM
COST = pl.CostEstimate(flops=1, bytes_accessed=1, transcendentals=0)
PARAMS = pltpu.CompilerParams(vmem_limit_bytes=16 * 2**20)
f32, i32 = jnp.float32, jnp.int32


def from_behind(block, axis, distance):
    devices = range(lax.axis_size(axis))
    route = [((i - distance) % len(devices), i) for i in devices]
    return lax.ppermute(block, axis, route)


def swapped(block, mask):
    route = [(i, i ^ mask) for i in range(lax.axis_size("spc"))]
    return lax.ppermute(block, "spc", route)


def any_specs(count):
    return [pl.BlockSpec(memory_space=pl.ANY)] * count


def along_lanes(values, index):
    return jnp.take_along_axis(values, index, axis=1, mode="promise_in_bounds")


def along_cells(values, index):
    return jnp.take_along_axis(values, index, axis=0, mode="promise_in_bounds")


def vreg_iota(dim):
    return lax.broadcasted_iota(i32, (8, ROWS), dim)


def padded(rows):
    return -(-rows // 8) * 8


def packing(needed):
    ones = jnp.where(needed, 1.0, 0.0).astype(jnp.bfloat16)
    row = lax.broadcasted_iota(i32, (ROWS, ROWS), 0)
    lane = lax.broadcasted_iota(i32, (ROWS, ROWS), 1)
    upto = jnp.where(row <= lane, 1.0, 0.0).astype(jnp.bfloat16)
    ranked = jnp.dot(ones, upto, preferred_element_type=f32).astype(i32)
    count = jnp.sum(jnp.where(needed, 1, 0), axis=1, keepdims=True)
    offsets, running = [], jnp.zeros((1, 1), i32)
    for cell in range(CELLS):
        offsets.append(running)
        running = running + count[cell : cell + 1]
    ends = offsets[1:] + [running]
    offset = jnp.concatenate(offsets, axis=0)
    lanes = lax.broadcasted_iota(i32, (CELLS, ROWS), 1)
    heights = lax.broadcasted_iota(i32, (CELLS, ROWS), 0)
    flat = offset + ranked - 1
    unpack_lane = flat & 127
    unpack_row = (offset >> 7) + jnp.where(lanes < (offset & 127), 1, 0)
    place = heights * ROWS + lanes
    pack_row = jnp.zeros((CELLS, ROWS), i32)
    for cell in range(CELLS):
        pack_row = pack_row + jnp.where(place >= ends[cell], 1, 0)
    pack_row = jnp.minimum(pack_row, CELLS - 1)
    wanted = (lanes - offset) & 127
    halves = []
    for half in range(2):
        at = slice(8 * half, 8 * half + 8)
        position = jnp.zeros((8, ROWS), i32)
        for step in (64, 32, 16, 8, 4, 2, 1):
            probe = along_lanes(ranked[at], position + (step - 1))
            position = jnp.where(probe <= wanted[at], position + step, position)
        halves.append(position)
    return (jnp.concatenate(halves, axis=0), pack_row, unpack_row, unpack_lane), running


def tables_kernel(shifts_ref, near_ref, polar_ref, which_ref):
    shifts = jnp.broadcast_to(shifts_ref[...], (CELLS, ROWS))
    cell = lax.broadcasted_iota(i32, (CELLS, ROWS), 0)
    needed = jnp.where(
        shifts < CELLS, jnp.where(cell <= shifts, 1, 0),
        jnp.where((cell == 0) | (cell > shifts - CELLS), 1, 0),
    ) > 0
    made, near_cells = packing(needed)
    for at, table in enumerate(made):
        near_ref[CELLS * at : CELLS * at + CELLS, :] = table
    within = vreg_iota(1) & (POLAR - 1)
    folded = along_lanes(shifts[:8], within)
    folded = jnp.concatenate([folded, folded], axis=0)
    needed = cell <= folded - CELLS
    (pack_lane, pack_row, unpack_row, unpack_lane), polar_cells = packing(needed)
    near_cells, polar_cells = jnp.sum(near_cells), jnp.sum(polar_cells)
    which_ref[0] = sum(
        jnp.where((near_cells > ROWS * (8 + a)) | (polar_cells > ROWS * (8 + c)), 1, 0)
        for a, c in SPARES[:-1]
    )
    polar_ref[0:16, :] = pack_lane
    polar_ref[16:32, :] = pack_row
    polar_ref[32:48, :] = unpack_row
    for level in range(LEVELS):
        for half in range(2):
            start = 48 + CELLS * level + 8 * half
            polar_ref[start : start + 8, :] = along_lanes(
                unpack_lane[8 * half : 8 * half + 8], within + POLAR * level
            )


def make_tables(shifts):
    return pl.pallas_call(
        tables_kernel,
        out_shape=(
            jax.ShapeDtypeStruct((4 * CELLS, ROWS), i32),
            jax.ShapeDtypeStruct((3 * CELLS + LEVELS * CELLS, ROWS), i32),
            jax.ShapeDtypeStruct((1,), i32),
        ),
        out_specs=(
            pl.BlockSpec(memory_space=VMEM),
            pl.BlockSpec(memory_space=VMEM),
            pl.BlockSpec(memory_space=pltpu.SMEM),
        ),
        name="tables",
        compiler_params=PARAMS,
    )(shifts)


def turning(shifts):
    back = vreg_iota(0) - shifts - 1
    return back & 7, (back & 15) >= 8


def turned(low, high, turn):
    index, swap = turn
    low, high = along_cells(low, index), along_cells(high, index)
    return jnp.where(swap, high, low), jnp.where(swap, low, high)


def far_masks(shifts):
    cell = vreg_iota(0)
    masks = []
    for half in range(2):
        at = cell + 8 * half
        polar = at <= shifts - CELLS
        behind = at <= shifts
        masks.append((behind, polar))
    return masks


def near_of(far, first):
    last = vreg_iota(0) == 7
    rolled = [pltpu.roll(half, 7, 0) for half in (far[0], far[1], first)]
    return (
        jnp.where(last, rolled[1], rolled[0]),
        jnp.where(last, rolled[2], rolled[1]),
    )


def table(ref, which, half):
    begin = CELLS * which + 8 * half
    return ref[begin : begin + 8, :]


def packer(table_ref, spare):
    lanes = (table(table_ref, 0, 0), table(table_ref, 0, 1))
    rows = table(table_ref, 1, 0)
    later = jnp.maximum(table(table_ref, 1, 1) - 8, 0)
    early, rows = rows < 8, rows & 7

    def pack_plane(low, high):
        low, high = along_lanes(low, lanes[0]), along_lanes(high, lanes[1])
        main = jnp.where(early, along_cells(low, rows), along_cells(high, rows))
        return main, along_cells(high, later) if spare else None

    return pack_plane


def folded_in(before, plane, place):
    if before is None:
        return list(plane)
    here = vreg_iota(1) >= POLAR * place
    return [
        jnp.where(here, pltpu.roll(half, POLAR * place, 1), old)
        for half, old in zip(plane, before)
    ]


def put_extra(ref, lead, begin, spare, extra):
    if spare == 8:
        ref[(*lead, pl.ds(pl.multiple_of(begin, 8), 8), slice(None))] = extra
    else:
        for row in range(spare):
            ref[(*lead, pl.ds(begin + row, 1), slice(None))] = extra[row : row + 1]


def get_extra(ref, lead, begin, spare):
    if spare == 8:
        return [ref[(*lead, pl.ds(pl.multiple_of(begin, 8), 8), slice(None))]]
    return [
        jnp.broadcast_to(ref[(*lead, pl.ds(begin + row, 1), slice(None))], (8, ROWS))
        for row in range(spare)
    ]


def liner(table_ref, spare):
    row0, row1 = table(table_ref, 2, 0) & 7, table(table_ref, 2, 1)
    low_row, late_row = row1 & 7, row1 >= 8

    def lines(main, extra):
        low, high = along_cells(main, row0), along_cells(main, low_row)
        if spare == 8:
            high = jnp.where(late_row, along_cells(extra[0], low_row), high)
        else:
            for row, late in enumerate(extra):
                high = jnp.where(row1 == 8 + row, late, high)
        return [low, high]

    return lines


def far_of(own, behind, beyond, masks):
    return [
        jnp.where(masks[h][1], beyond[h], jnp.where(masks[h][0], behind[h], own[h]))
        for h in range(2)
    ]


def species_kernel(me_ref, shifts_ref, loads_ref, after_ref, keep_ref, send_ref):
    del after_ref
    shifts = jnp.broadcast_to(shifts_ref[...], (8, ROWS))
    turn = turning(shifts)
    species = loads_ref.shape[0]

    def body(b, carry):
        for away, (part, at) in enumerate(((keep_ref, 0), (send_ref, 0), (keep_ref, 1), (send_ref, 1))):
            level = jnp.bitwise_xor(me_ref[0], away)
            low = sum(loads_ref[s, b, level, 0:8, :] for s in range(1, species))
            high = sum(loads_ref[s, b, level, 8:16, :] for s in range(1, species))
            low = low + loads_ref[0, b, level, 0:8, :]
            high = high + loads_ref[0, b, level, 8:16, :]
            low, high = turned(low, high, turn)
            part[at, b, 0:8, :] = low
            part[at, b, 8:16, :] = high
        return carry

    lax.fori_loop(0, BINS, body, 0)


def species_sums(me, shifts, loads, after):
    return pl.pallas_call(
        species_kernel,
        out_shape=(jax.ShapeDtypeStruct((2, BINS, CELLS, ROWS), f32),) * 2,
        in_specs=[
            pl.BlockSpec(memory_space=pltpu.SMEM),
            pl.BlockSpec(memory_space=VMEM),
            pl.BlockSpec(memory_space=VMEM),
        ]
        + any_specs(1),
        out_specs=(pl.BlockSpec(memory_space=VMEM),) * 2,
        name="species_sums",
        compiler_params=PARAMS,
        cost_estimate=COST,
    )(me, shifts, loads, after)


PLANES = 2 * BINS
SUMS = PLANES * CELLS
FOLDS = -(-PLANES // LEVELS)


def chip_kernel(keep_ref, got_ref, frac_ref, east_ref, temp_ref, out_ref):
    for at in range(2):
        for b in range(BINS):
            begin = CELLS * (BINS * at + b)
            out_ref[begin : begin + CELLS, :] = keep_ref[at, b] + got_ref[at, b]
    frac = (frac_ref[0, 0:8, :], frac_ref[0, 8:16, :])
    east = near_of(frac, jnp.broadcast_to(east_ref[0], (8, ROWS)))
    for half in range(2):
        begin = SUMS + 8 * half
        out_ref[begin : begin + 8, :] = 1.0 - east[half]
        out_ref[begin + 16 : begin + 24, :] = frac[half]
        out_ref[begin + 32 : begin + 40, :] = temp_ref[0, 8 * half : 8 * half + 8, :]


def chip_sums(keep, got, frac, east, temp):
    return pl.pallas_call(
        chip_kernel,
        out_shape=jax.ShapeDtypeStruct((SUMS + 3 * CELLS, ROWS), f32),
        in_specs=[pl.BlockSpec(memory_space=VMEM)] * 5,
        out_specs=pl.BlockSpec(memory_space=VMEM),
        name="chip_sums",
        compiler_params=PARAMS,
        cost_estimate=COST,
    )(keep, got, frac, east, temp)


def all_kernel(spare, polar_spare, near_ref, polar_ref, mine_ref, other_ref, own_ref, ahead_ref, beyond_ref):
    pack_near, pack_polar = packer(near_ref, spare), packer(polar_ref, polar_spare)
    folded = None
    for plane in range(PLANES):
        begin = CELLS * plane
        across = CELLS * ((plane + BINS) % PLANES)
        low = mine_ref[begin : begin + 8, :] + other_ref[across : across + 8, :]
        high = mine_ref[begin + 8 : begin + 16, :] + other_ref[across + 8 : across + 16, :]
        own_ref[begin : begin + 8, :] = low
        own_ref[begin + 8 : begin + 16, :] = high
        main, extra = pack_near(low, high)
        ahead_ref[8 * plane : 8 * plane + 8, :] = main
        put_extra(ahead_ref, (), 8 * PLANES + plane * spare, spare, extra)
        place = plane % LEVELS
        folded = folded_in(folded if place else None, (low, high), place)
        if place == LEVELS - 1 or plane == PLANES - 1:
            fold = plane // LEVELS
            main, extra = pack_polar(*folded)
            beyond_ref[8 * fold : 8 * fold + 8, :] = main
            put_extra(beyond_ref, (), 8 * FOLDS + fold * polar_spare, polar_spare, extra)


def all_sums(spares, near_table, polar_table, mine, other):
    spare, polar_spare = spares
    return pl.pallas_call(
        functools.partial(all_kernel, spare, polar_spare),
        out_shape=(
            jax.ShapeDtypeStruct((SUMS, ROWS), f32),
            jax.ShapeDtypeStruct((padded((8 + spare) * PLANES), ROWS), f32),
            jax.ShapeDtypeStruct(((8 + polar_spare) * FOLDS, ROWS), f32),
        ),
        in_specs=[pl.BlockSpec(memory_space=VMEM)] * 4,
        out_specs=(pl.BlockSpec(memory_space=VMEM),) * 3,
        name="all_sums",
        compiler_params=PARAMS,
        cost_estimate=COST,
    )(near_table, polar_table, mine, other)


def organic_kernel(
    spare, polar_spare,
    shifts_ref, near_ref, polar_ref, own_ref, behind_ref, beyond_ref, mine_ref, other_ref, after_ref,
    out_ref,
):
    del after_ref
    shifts = jnp.broadcast_to(shifts_ref[...], (8, ROWS))
    masks = far_masks(shifts)
    is_polar = shifts >= CELLS
    near_lines, polar_lines = liner(near_ref, spare), liner(polar_ref, polar_spare)
    lanes = (table(near_ref, 3, 0), table(near_ref, 3, 1))
    spread = None
    for at, meta_ref in enumerate((mine_ref, other_ref)):
        meta = [
            [meta_ref[SUMS + 16 * n + 8 * h : SUMS + 16 * n + 8 * h + 8, :] for h in range(2)]
            for n in range(3)
        ]
        rest, frac, temp = meta
        advected = []
        for b in range(BINS):
            plane = BINS * at + b
            begin, fold, place = CELLS * plane, plane // LEVELS, plane % LEVELS
            own = (own_ref[begin : begin + 8, :], own_ref[begin + 8 : begin + 16, :])
            if place == 0:
                spread = polar_lines(
                    beyond_ref[8 * fold : 8 * fold + 8, :],
                    get_extra(beyond_ref, (), 8 * FOLDS + fold * polar_spare, polar_spare),
                )
            lines = near_lines(
                behind_ref[8 * plane : 8 * plane + 8, :],
                get_extra(behind_ref, (), 8 * PLANES + plane * spare, spare),
            )
            behind = [along_lanes(lines[h], lanes[h]) for h in range(2)]
            beyond = [along_lanes(spread[h], table(polar_ref, 3 + place, h)) for h in range(2)]
            far = far_of(own, behind, beyond, masks)
            near = near_of(far, jnp.where(is_polar, behind[0], own[0]))
            advected.append([rest[h] * near[h] + frac[h] * far[h] for h in range(2)])
        for half in range(2):
            base = (298.15 / temp[half]) * jnp.exp(
                HEAT_OF_BOILING * (1.0 / 298.15 - 1.0 / temp[half])
            )
            organic = SEED + sum(advected[b][half] for b in range(BINS))
            for _ in range(PITERS):
                ratio = base / organic
                organic = SEED + sum(
                    advected[b][half] / (1.0 + 10.0 ** (b - 3) * ratio) for b in range(BINS)
                )
            out_ref[at, 8 * half : 8 * half + 8, :] = rest[half]
            out_ref[at, 16 + 8 * half : 24 + 8 * half, :] = frac[half]
            out_ref[at, 32 + 8 * half : 40 + 8 * half, :] = base / organic


def organic_of(spares, shifts, near_table, polar_table, own, behind, beyond, mine, other, after):
    return pl.pallas_call(
        functools.partial(organic_kernel, *spares),
        out_shape=jax.ShapeDtypeStruct((2, 3 * CELLS, ROWS), f32),
        in_specs=[pl.BlockSpec(memory_space=VMEM)] * 8 + any_specs(1),
        out_specs=pl.BlockSpec(memory_space=VMEM),
        name="organic",
        compiler_params=PARAMS,
        cost_estimate=COST,
    )(shifts, near_table, polar_table, own, behind, beyond, mine, other, after)


def pack_kernel(
    spare, polar_spare, start, shifts_ref, near_ref, polar_ref, loads_ref, *rest
):
    ahead_ref, beyond_ref = rest[-2:]
    shifts = jnp.broadcast_to(shifts_ref[...], (8, ROWS))
    turn = turning(shifts)
    s = pl.program_id(0) + start

    pack_near, pack_polar = packer(near_ref, spare), packer(polar_ref, polar_spare)

    def body(b, totals):
        folded, sums = None, []
        for level in range(LEVELS):
            low, high = turned(
                loads_ref[s, b, level, 0:8, :], loads_ref[s, b, level, 8:16, :], turn
            )
            sums.append(totals[level] + (low + high))
            folded = folded_in(folded, (low, high), level)
            main, extra = pack_near(low, high)
            plane = b * LEVELS + level
            ahead_ref[0, pl.ds(pl.multiple_of(8 * plane, 8), 8), :] = main
            put_extra(ahead_ref, (0,), 8 * BINS * LEVELS + plane * spare, spare, extra)
        main, extra = pack_polar(*folded)
        beyond_ref[0, pl.ds(pl.multiple_of(8 * b, 8), 8), :] = main
        put_extra(beyond_ref, (0,), 8 * BINS + b * polar_spare, polar_spare, extra)
        return tuple(sums)

    totals = lax.fori_loop(0, BINS, body, (jnp.zeros((8, ROWS), f32),) * LEVELS, unroll=3)
    begin = (8 + spare) * BINS * LEVELS
    for level in range(LEVELS):
        ahead_ref[0, begin + level : begin + level + 1, :] = jnp.sum(
            totals[level], axis=0, keepdims=True
        )


def packed_rows(spare, polar_spare):
    return (
        padded((8 + spare) * BINS * LEVELS + LEVELS),
        (8 + polar_spare) * BINS,
    )


def whole_spec(shape):
    return pl.BlockSpec(shape, lambda i: (0,) * len(shape))


def pack(spares, start, count, shifts, near_table, polar_table, loads, after, before):
    rows, polar_rows = packed_rows(*spares)
    species = loads.shape[0]
    args = [shifts, near_table, polar_table, loads, *after]
    in_specs = [pl.BlockSpec(memory_space=VMEM)] * 4 + any_specs(len(after))
    aliases = {}
    if before is not None:
        aliases = {len(args): 1}
        args.append(before)
        in_specs.append(pl.BlockSpec(memory_space=pl.ANY))
    return pl.pallas_call(
        functools.partial(pack_kernel, *spares, start),
        grid=(count,),
        out_shape=(
            jax.ShapeDtypeStruct((count, rows, ROWS), f32),
            jax.ShapeDtypeStruct((species, polar_rows, ROWS), f32),
        ),
        in_specs=in_specs,
        out_specs=(
            pl.BlockSpec((1, rows, ROWS), lambda i: (i, 0, 0)),
            pl.BlockSpec((1, polar_rows, ROWS), lambda i: (i + start, 0, 0)),
        ),
        input_output_aliases=aliases,
        name=f"pack_{start}",
        compiler_params=PARAMS,
        cost_estimate=COST,
    )(*args)


def weights_kernel(me_ref, pair_ref, other_ref, diff_ref, near_w, far_w, solve, fracs):
    for half in range(2):
        at = slice(8 * half, 8 * half + 8)
        diffusive = [diff_ref[k, at, :] for k in range(LEVELS - 1)]
        nothing = jnp.zeros((8, ROWS), f32)
        lower = [nothing] + diffusive
        upper = diffusive + [nothing]
        previous = nothing
        for k in range(LEVELS):
            pivot = 1.0 + lower[k] + upper[k] - lower[k] * previous
            inverse = 1.0 / pivot
            previous = upper[k] * inverse
            solve[0, k, at, :] = inverse
            solve[1, k, at, :] = lower[k] * inverse
            solve[2, k, at, :] = previous
    for away in range(LEVELS):
        level_ref = (pair_ref, other_ref)[away & 1].at[away >> 1]
        level = jnp.bitwise_xor(me_ref[0], away)
        for half in range(2):
            at = slice(8 * half, 8 * half + 8)
            rest_of = level_ref[8 * half : 8 * half + 8, :]
            frac = level_ref[16 + 8 * half : 24 + 8 * half, :]
            ratio = level_ref[32 + 8 * half : 40 + 8 * half, :]
            fracs[level, at, :] = frac
            inverse = solve[0, level, at, :]
            near_top, far_top = rest_of * inverse, frac * inverse
            for b in range(BINS):
                weight = 1.0 / (1.0 + 10.0 ** (b - 3) * ratio)
                near_w[b, level, at, :] = near_top * weight
                far_w[b, level, at, :] = far_top * weight


def weights_of(me, pair, other, diffusive):
    block = (LEVELS, CELLS, ROWS)
    return pl.pallas_call(
        weights_kernel,
        out_shape=tuple(
            jax.ShapeDtypeStruct(shape, f32)
            for shape in ((BINS,) + block, (BINS,) + block, (3,) + block, block)
        ),
        in_specs=[pl.BlockSpec(memory_space=pltpu.SMEM)] + [pl.BlockSpec(memory_space=VMEM)] * 3,
        out_specs=(pl.BlockSpec(memory_space=VMEM),) * 4,
        name="weights",
        compiler_params=PARAMS,
        cost_estimate=COST,
    )(me, pair, other, diffusive)


def final_kernel(
    spare, polar_spare, start,
    shifts_ref, near_ref, polar_ref, near_w, far_w, solve, fracs, loads_ref, behind_ref, beyond_ref,
    *rest,
):
    particle_ref, flux_ref = rest[-2:]
    shifts = jnp.broadcast_to(shifts_ref[...], (8, ROWS))
    halves = (slice(0, 8), slice(8, 16))
    turn = turning(shifts)
    masks = far_masks(shifts)
    is_polar = shifts >= CELLS
    i = pl.program_id(0)
    s = i + start

    near_lines, polar_lines = liner(near_ref, spare), liner(polar_ref, polar_spare)
    lanes = (table(near_ref, 3, 0), table(near_ref, 3, 1))

    def body(b, carry):
        spread = polar_lines(
            beyond_ref[s, pl.ds(pl.multiple_of(8 * b, 8), 8), :],
            get_extra(beyond_ref, (s,), 8 * BINS + b * polar_spare, polar_spare),
        )
        forward = [None] * LEVELS
        previous = None
        sums = []
        for k in range(LEVELS):
            low, high = loads_ref[s, b, k, 0:8, :], loads_ref[s, b, k, 8:16, :]
            own = turned(low, high, turn)
            plane = b * LEVELS + k
            lines = near_lines(
                behind_ref[i, pl.ds(pl.multiple_of(8 * plane, 8), 8), :],
                get_extra(behind_ref, (i,), 8 * BINS * LEVELS + plane * spare, spare),
            )
            behind = [along_lanes(lines[h], lanes[h]) for h in range(2)]
            beyond = [along_lanes(spread[h], table(polar_ref, 3 + k, h)) for h in range(2)]
            far = far_of(own, behind, beyond, masks)
            first = jnp.where(is_polar, behind[0], own[0])
            near = near_of(far, first)
            terms = (far[0], far[1], first, low, high)
            sums.append(tuple(a + t for a, t in zip(carry[k], terms)))
            step = []
            for half, at in enumerate(halves):
                value = near_w[b, k, at, :] * near[half] + far_w[b, k, at, :] * far[half]
                if k:
                    value = value + solve[1, k, at, :] * previous[half]
                step.append(value)
            forward[k] = previous = step
        following = forward[LEVELS - 1]
        for half, at in enumerate(halves):
            particle_ref[0, b, LEVELS - 1, at, :] = following[half]
        for k in range(LEVELS - 2, -1, -1):
            following = [
                forward[k][half] + solve[2, k, at, :] * following[half]
                for half, at in enumerate(halves)
            ]
            for half, at in enumerate(halves):
                particle_ref[0, b, k, at, :] = following[half]
        return tuple(sums)

    zero = jnp.zeros((8, ROWS), f32)
    sums = lax.fori_loop(0, BINS, body, ((zero,) * 5,) * LEVELS, unroll=3)
    cell = vreg_iota(0)
    within = shifts & (CELLS - 1)
    for k in range(LEVELS):
        far0, far1, first, low, high = sums[k]
        near0, near1 = near_of((far0, far1), first)
        counted = jnp.where((cell >= 1) & (cell <= within), far0, 0.0) + jnp.where(
            cell + 8 <= within, far1, 0.0
        )
        window = jnp.sum(counted, axis=0, keepdims=True)
        begin = (8 + spare) * BINS * LEVELS + k
        window = window + jnp.where(
            shifts_ref[...] >= CELLS, behind_ref[i, begin : begin + 1, :], 0.0
        )
        base = jnp.broadcast_to(window, (8, ROWS))
        for half, (gained, lost, far) in enumerate(((low, near0, far0), (high, near1, far1))):
            change = gained - lost
            running = change
            for step in (1, 2, 4):
                running = running + jnp.where(cell >= step, pltpu.roll(running, step, 0), 0.0)
            at = halves[half]
            flux_ref[0, k, at, :] = base + (running - change) + fracs[k, at, :] * far
            if half == 0:
                base = base + jnp.broadcast_to(running[7:8, :], (8, ROWS))


def final(
    spares, start, count, shifts, near_table, polar_table, weights, loads, behind, beyond, before
):
    species = loads.shape[0]
    outs = (
        jax.ShapeDtypeStruct((species, BINS, LEVELS, CELLS, ROWS), f32),
        jax.ShapeDtypeStruct((species, LEVELS, CELLS, ROWS), f32),
    )
    args = [shifts, near_table, polar_table, *weights, loads, behind, beyond]
    in_specs = [pl.BlockSpec(memory_space=VMEM)] * len(args)
    aliases = {}
    if before is not None:
        aliases = {len(args): 0, len(args) + 1: 1}
        args += list(before)
        in_specs += [pl.BlockSpec(memory_space=pl.ANY)] * 2
    return pl.pallas_call(
        functools.partial(final_kernel, *spares, start),
        grid=(count,),
        out_shape=outs,
        in_specs=in_specs,
        out_specs=(
            pl.BlockSpec((1, BINS, LEVELS, CELLS, ROWS), lambda i: (i + start, 0, 0, 0, 0)),
            pl.BlockSpec((1, LEVELS, CELLS, ROWS), lambda i: (i + start, 0, 0, 0)),
        ),
        input_output_aliases=aliases,
        name=f"final_{start}",
        compiler_params=PARAMS,
        cost_estimate=COST,
    )(*args)


def along_meridian(block):
    size = lax.axis_size("lon")
    return lax.ppermute(block, "lon", [(i, (i + 2) % size) for i in range(1, size, 2)])


def crossed(block):
    return lax.ppermute(block, "lon", [(i, i ^ 1) for i in range(lax.axis_size("lon"))])


def pipeline(spares, me, shifts, near_table, polar_table, loads, frac, temp, diffusive):
    tables = (shifts, near_table, polar_table)
    odd = lax.axis_index("lon") % 2 == 1
    starts = [sum(CHUNKS[:i]) for i in range(len(CHUNKS))]
    last = len(CHUNKS) - 1
    east = from_behind(frac[:, :1, :], "lon", -1)
    keep, send = species_sums(me, shifts, loads, near_table)
    got = swapped(send, 1)
    mine = chip_sums(keep, got, frac, east, temp)
    other = swapped(mine, 2)
    after, beyond, aheads = [keep], None, [None] * len(CHUNKS)
    for at in (0, last, 2, 1):
        aheads[at], beyond = pack(
            spares, starts[at], CHUNKS[at], *tables, loads, after, beyond
        )
        after = [aheads[at]]
    other, aheads[1], beyond = lax.optimization_barrier((other, aheads[1], beyond))
    own, ahead_sums, beyond_sums = all_sums(spares, near_table, polar_table, mine, other)
    relayed = along_meridian(aheads[last])
    aheads[0], _ = lax.optimization_barrier((aheads[0], mine))
    sums_behind = from_behind(ahead_sums, "lon", 1)
    sums_beyond = from_behind(beyond_sums, "lon", 2)
    aheads[1], sums_beyond = lax.optimization_barrier((aheads[1], sums_beyond))
    behind = [from_behind(aheads[0], "lon", 1), from_behind(aheads[1], "lon", 1)]
    beyond = from_behind(beyond, "lon", 2)
    aheads[2], behind[0] = lax.optimization_barrier((aheads[2], behind[0]))
    behind.append(from_behind(aheads[2], "lon", 1))
    mixed, sums_behind, sums_beyond = lax.optimization_barrier(
        (jnp.where(odd, relayed, aheads[last]), sums_behind, sums_beyond)
    )
    behind.append(crossed(mixed))
    level = organic_of(spares, *tables, own, sums_behind, sums_beyond, mine, other, behind[0])
    weights = weights_of(me, level, swapped(level, 1), diffusive)
    outs = None
    for start, count, block in zip(starts, CHUNKS, behind):
        outs = final(spares, start, count, *tables, weights, loads, block, beyond, outs)
    return tuple(outs)


def per_device(loads, frac, temp, diffusive, whole_shifts):
    me = lax.axis_index("spc").astype(i32).reshape(1)
    shifts = whole_shifts.reshape(1, ROWS)
    near_table, polar_table, which = make_tables(shifts)
    branches = [functools.partial(pipeline, spares) for spares in SPARES]
    return lax.switch(
        which[0], branches, me, shifts, near_table, polar_table, loads, frac, temp, diffusive
    )


def solution(mesh):
    placed = (
        P("spc", None, None, "lon", None),
        P("spc", "lon", None),
        P("spc", "lon", None),
        P(None, "lon", None),
        P(),
    )
    return jax.shard_map(
        per_device,
        mesh=mesh,
        in_specs=placed,
        out_specs=(P("spc", None, None, "lon", None), P("spc", None, "lon", None)),
        check_vma=False,
    )
```
